256 devices in a mesh: scene: 8 (over x, core), seq: 32 (over y, z).
Axes of the slice: x: 4, y: 4, z: 8, core: 2. Of those that a mesh axis runs over, the one named last changes fastest.
Arguments:
- tokens: bfloat16 [4096, 64, 512], P(('scene', 'seq')), parts along dimension 0, may hold values from -6 to 6
- block_counts: int32 [256], P('scene'), parts along dimension 0, may hold values from 1 to 16, 320 in all
- gains: float32 [3, 512], replicated, may hold values from 0.1 to 1.9
- qkv_time: bfloat16 [512, 1536], replicated, may hold values from -0.25 to 0.25
- out_time: bfloat16 [512, 512], replicated, may hold values from -0.25 to 0.25
- qkv_scene: bfloat16 [512, 1536], replicated, may hold values from -0.25 to 0.25
- out_scene: bfloat16 [512, 512], replicated, may hold values from -0.25 to 0.25
- mlp_in: bfloat16 [512, 2048], replicated, may hold values from -0.25 to 0.25
- mlp_out: bfloat16 [2048, 512], replicated, may hold values from -0.125 to 0.125
Outputs:
- encoded: bfloat16 [4096, 64, 512], P(('scene', 'seq')), parts along dimension 0
The draws below stay inside these ranges and needn't reach their ends.
There are 8 independent parts, one for each index of `scene`. The reference program is written for one: setup_inputs(seed, part) draws one part's arguments, and reference() takes and returns one part's arrays. A program takes and returns all parts, laid end to end along the dimension named above; an argument that names none is the same for every part. Nothing has to cross between parts.
Inputs may be any that keep to these rules, and one draw needn't show every extreme that they name: Within each scene, the live agents of each aligned block of 16 slots are its first block_counts slots, the scene's counts sum to 320, and some block of the scene is full.
All inputs are finite; a program needn't handle non-finite values.
Results may differ from the reference program's by a relative error of at most 0.02.
Values may be sent and summed in bfloat16 or wider, within the bound.
No kernel may reach another device: no remote copies, remote signals or barrier semaphores. Data moves between devices by JAX's collectives and lax.ppermute only.
A program may use at most 128 MiB of HBM per device.

```python
import math
import jax
import jax.numpy as jnp
import numpy as np
from jax import lax

D = 512
HEADS = 8
FF = 2048
AG_DEV = 16
STEPS = 64
AGENTS = 512
N_SEQ = 32


def levels(rng, extent, pieces, smallest, high):
    def one(dim, blocks):
        heights = jax.random.uniform(jax.random.fold_in(jax.random.fold_in(rng, 6), dim), (blocks,), jnp.float32, smallest / len(pieces), high / len(pieces))
        return jnp.repeat(jnp.exp(heights), extent[dim] // blocks).reshape((-1,) + (1,) * (len(extent) - dim - 1))

    factor_of = one(*pieces[0])
    for cut in pieces[1:]:
        factor_of = factor_of * one(*cut)
    return factor_of


def profile(amount, total, bound, skew):
    weights = [(1 << 20) // math.isqrt(grade ** skew) + 1 for grade in range(2, amount + 1)]
    rest, given = total - bound - (amount - 1), [1] * (amount - 1)
    while rest > 0:
        movable = [i for i in range(amount - 1) if given[i] < bound]
        pool, left = sum([weights[i] for i in movable]), rest
        for i in movable:
            more = min(bound - given[i], max(1, left * weights[i] // pool), rest)
            given[i] = given[i] + more
            rest = rest - more
    return np.array([bound] + given)


def ragged(stream_key, number_of, total, reach, slope):
    if number_of == 2:
        one = jax.random.randint(stream_key, (), max(1, total - reach), min(reach, total - 1) + 1)
        return jnp.stack([one, total - one])
    sizes = jnp.asarray(profile(number_of, total, reach, slope), jnp.int32)
    couples = (number_of - 1) // 2
    source_of, sink = sizes[1:1 + 2 * couples:2], sizes[2:2 + 2 * couples:2]
    margin = jnp.minimum(source_of - 1, reach - sink)
    shifted = jax.random.randint(jax.random.fold_in(stream_key, 1), (couples,), 0, 1 << 20) % (margin + 1)
    sizes = sizes.at[1:1 + 2 * couples:2].set(source_of - shifted).at[2:2 + 2 * couples:2].set(sink + shifted)
    return sizes[jax.random.permutation(jax.random.fold_in(stream_key, 2), number_of)]


def noise(key, extent, width, reach, pieces=(), kind=jnp.bfloat16):
    loudness = levels(key, extent, pieces, -0.22, 0.18) if pieces else 1.0
    entries = jax.random.normal(key, extent, jnp.float32) * width * loudness
    return jnp.minimum(jnp.maximum(entries, -reach), reach).astype(kind)


def setup_inputs(seed: int = 0, part: int = 0) -> dict:
    streams_of = jax.random.split(jax.random.key(seed), 10)
    part_keys = jax.random.split(jax.random.fold_in(streams_of[9], part), 10)
    tokens = noise(part_keys[0], (AGENTS, STEPS, D), 1.0, 6.0, ((0, 32),))
    block_counts = ragged(part_keys[1], N_SEQ, AG_DEV * N_SEQ * 5 // 8, AG_DEV, 2).astype(jnp.int32)
    gains = jnp.clip(1.0 + 0.18 * jax.random.normal(streams_of[2], (3, D), jnp.float32), 0.1, 1.9)
    qkv_time = noise(streams_of[3], (D, 3 * D), D ** -0.5, 0.25)
    out_time = noise(streams_of[4], (D, D), D ** -0.5, 0.25)
    qkv_scene = noise(streams_of[5], (D, 3 * D), D ** -0.5, 0.25)
    out_scene = noise(streams_of[6], (D, D), D ** -0.5, 0.25)
    mlp_in = noise(streams_of[7], (D, FF), D ** -0.5, 0.25)
    mlp_out = noise(streams_of[8], (FF, D), FF ** -0.5, 0.125)
    return {"tokens": tokens, "block_counts": block_counts, "gains": gains, "qkv_time": qkv_time, "out_time": out_time, "qkv_scene": qkv_scene, "out_scene": out_scene, "mlp_in": mlp_in, "mlp_out": mlp_out}


def rms_norm(values, gain):
    floats = values.astype(jnp.float32)
    inverse = lax.rsqrt(lax.optimization_barrier(jnp.mean(floats * floats, axis=-1, keepdims=True)) + 1e-06)
    return (floats * inverse * gain).astype(jnp.bfloat16)

def reference(tokens, block_counts, gains, qkv_time, out_time, qkv_scene, out_scene, mlp_in, mlp_out):
    agents, step_count, model_width = tokens.shape
    head_size = model_width // HEADS
    inv_root = 1.0 / float(head_size) ** 0.5
    slot_ids = jnp.arange(agents, dtype=jnp.int32)
    is_live = slot_ids % AG_DEV < jnp.repeat(block_counts, AG_DEV)
    rows = agents * step_count
    first = rms_norm(tokens, gains[0])
    packed = jnp.dot(first.reshape(rows, model_width), qkv_time, preferred_element_type=jnp.float32)
    packed = packed.astype(jnp.bfloat16).reshape(agents, step_count, 3, HEADS, head_size).astype(jnp.float32)
    scores = jnp.einsum('ashd,athd->ahst', packed[:, :, 0], packed[:, :, 1]) * inv_root
    weights = jax.nn.softmax(scores, axis=-1).astype(jnp.bfloat16)
    context = jnp.einsum('ahst,athd->ashd', weights.astype(jnp.float32), packed[:, :, 2]).astype(jnp.bfloat16)
    update = jnp.dot(context.reshape(rows, model_width), out_time, preferred_element_type=jnp.float32)
    after_time = (tokens.astype(jnp.float32) + update.reshape(agents, step_count, model_width)).astype(jnp.bfloat16)
    second = rms_norm(after_time, gains[1])
    packed_two = jnp.dot(second.reshape(rows, model_width), qkv_scene, preferred_element_type=jnp.float32)
    packed_two = packed_two.astype(jnp.bfloat16).reshape(agents, step_count, 3, HEADS, head_size)
    per_step = jnp.transpose(packed_two, (1, 0, 2, 3, 4))

    def spatial(item):
        floats = item.astype(jnp.float32)
        logits = jnp.einsum('ahd,bhd->hab', floats[:, 0], floats[:, 1]) * inv_root
        logits = jnp.where(is_live[None, None, :], logits, -1e+30)
        probs = jax.nn.softmax(logits, axis=-1).astype(jnp.bfloat16)
        mixed_ctx = jnp.einsum('hab,bhd->ahd', probs.astype(jnp.float32), floats[:, 2]).astype(jnp.bfloat16)
        return jnp.dot(mixed_ctx.reshape(agents, model_width), out_scene, preferred_element_type=jnp.float32).astype(jnp.bfloat16)
    scene_out = jnp.transpose(lax.map(spatial, per_step), (1, 0, 2))
    after_scene = (after_time.astype(jnp.float32) + scene_out.astype(jnp.float32)).astype(jnp.bfloat16)
    third = rms_norm(after_scene, gains[2])
    hidden = jnp.maximum(jnp.dot(third.reshape(rows, model_width), mlp_in, preferred_element_type=jnp.float32), 0.0).astype(jnp.bfloat16)
    result = after_scene.astype(jnp.float32) + jnp.dot(hidden, mlp_out, preferred_element_type=jnp.float32).reshape(agents, step_count, model_width)
    return jnp.where(is_live[:, None, None], result, 0.0).astype(jnp.bfloat16)
```

```python
import jax
import jax.numpy as jnp
from jax import lax
from jax.experimental import pallas as pl
from jax.experimental.pallas import tpu as pltpu
from jax.sharding import PartitionSpec as P

D = 512
FF = 2048
SLOTS = 16
STEPS = 64
GROUPS = 32
LOCAL = STEPS // GROUPS
AGENTS = SLOTS * GROUPS
LIVE = 320
GROUP = 4
ROWS = GROUP * STEPS
PAIR = 128
INV_ROOT = 0.125
BF16 = jnp.bfloat16
F32 = jnp.float32


def dot(a, b):
    return jnp.dot(a, b, preferred_element_type=F32)


def dot_nt(a, b):
    return lax.dot_general(a, b, (((1,), (1,)), ((), ())), preferred_element_type=F32)


def rms(values, gain):
    floats = values.astype(F32)
    inverse = lax.rsqrt(jnp.mean(floats * floats, axis=-1, keepdims=True) + 1e-06)
    return (floats * inverse * gain).astype(BF16)


def iota(shape, dim):
    return lax.broadcasted_iota(jnp.int32, shape, dim)


def regroup():
    row, col = iota((256, 256), 0), iota((256, 256), 1)
    return jnp.where(col == (row & 15) * 16 + (row >> 4), 1.0, 0.0).astype(BF16)


def head_split(q):
    low = iota(q.shape, 1) < 64
    q = q.astype(F32) * INV_ROOT
    first = jnp.where(low, q, 0.0)
    return jnp.concatenate([first, q - first], axis=0).astype(BF16)


def attend(scores, v):
    top = jnp.max(scores, axis=-1, keepdims=True)
    p = jnp.exp(scores - top).astype(BF16)
    both = dot(p, jnp.concatenate([v, jnp.ones_like(v)], axis=1))
    n = both.shape[0] // 2
    low = iota((n, PAIR), 1) < 64
    top_rows = both[:n]
    bottom = both[n:]
    value = jnp.where(low, top_rows[:, :PAIR], bottom[:, :PAIR])
    total = jnp.where(low, top_rows[:, PAIR:], bottom[:, PAIR:])
    return (value / total).astype(BF16)


def time_kernel(counts, tokens, gains, qkv_w, out_w, result, x1, ctx):
    step = pl.program_id(0)
    count = counts[lax.axis_index("seq")]
    first = step * GROUP

    @pl.when(first < count)
    def _():
        values = tokens[...].reshape(ROWS, D)
        packed = dot(rms(values, gains[0:1, :]), qkv_w[...]).astype(BF16)
        block = 2 * STEPS
        same = ((iota((2 * block, block), 0) >> 6) & 1) == (iota((2 * block, block), 1) >> 6)
        for pair in range(GROUP // 2):
            rows = slice(pair * block, (pair + 1) * block)
            for head in range(D // PAIR):
                low = head * PAIR
                q = packed[rows, low : low + PAIR]
                k = packed[rows, D + low : D + low + PAIR]
                v = packed[rows, 2 * D + low : 2 * D + low + PAIR]
                scores = jnp.where(same, dot_nt(head_split(q), k), -1e30)
                ctx[rows, low : low + PAIR] = attend(scores, v)
        update = dot(ctx[...], out_w[...])
        after = (values.astype(F32) + update).astype(BF16)
        x1[pl.ds(first, GROUP)] = after.reshape(GROUP, STEPS, D)

    @pl.when(first >= count)
    def _():
        x1[pl.ds(first, GROUP)] = jnp.zeros((GROUP, STEPS, D), BF16)

    @pl.when(step == SLOTS // GROUP - 1)
    def _():
        turn = regroup()
        for part in range(STEPS // 16):
            rows = x1[:, part * 16 : (part + 1) * 16, :].reshape(256, D)
            turned = dot(turn, rows).astype(BF16)
            many = 16 // LOCAL
            result[part * many : (part + 1) * many] = turned.reshape(many, LOCAL * SLOTS, D)


def time_part(counts, tokens, gains, qkv_w, out_w):
    whole = lambda *shape: pl.BlockSpec(shape, lambda i: (0,) * len(shape))
    return pl.pallas_call(
        time_kernel,
        grid=(SLOTS // GROUP,),
        in_specs=[
            pl.BlockSpec(memory_space=pltpu.SMEM),
            pl.BlockSpec((GROUP, STEPS, D), lambda i: (i, 0, 0)),
            whole(3, D),
            whole(D, 3 * D),
            whole(D, D),
        ],
        out_specs=whole(GROUPS, LOCAL * SLOTS, D),
        out_shape=jax.ShapeDtypeStruct((GROUPS, LOCAL * SLOTS, D), BF16),
        scratch_shapes=[pltpu.VMEM((SLOTS, STEPS, D), BF16), pltpu.VMEM((ROWS, D), BF16)],
        compiler_params=pltpu.CompilerParams(vmem_limit_bytes=32 << 20),
        cost_estimate=pl.CostEstimate(
            flops=6 << 30, bytes_accessed=4 << 20, transcendentals=1 << 20
        ),
        name="time_part",
    )(counts, tokens, gains, qkv_w, out_w)


def scene_kernel(
    counts, recv, gains, qkv_hbm, out_hbm, in_hbm, back_hbm, result,
    qkv_w, out_w, in_w, back_w, xs, packed, ctx, sems,
):
    sources = (qkv_hbm, out_hbm, in_hbm, back_hbm)
    copies = [
        pltpu.make_async_copy(source, target, sems.at[i])
        for i, (source, target) in enumerate(zip(sources, (qkv_w, out_w, in_w, back_w)))
    ]
    for copy in copies:
        copy.start()

    slot = iota((8, AGENTS), 1)
    inside = slot & 15
    place = jnp.full((8, AGENTS), -1, jnp.int32)
    offsets, offset = [], jnp.int32(0)
    for block in range(GROUPS):
        count = counts[block]
        here = ((slot >> 4) == block) & (inside < count)
        place = jnp.where(here, inside + offset, place)
        offsets.append((offset, count))
        offset = offset + count
    gather = jnp.where(iota((LIVE, AGENTS), 0) == place[0:1], 1.0, 0.0).astype(BF16)
    for local in range(LOCAL):
        x = recv[:, local * SLOTS : (local + 1) * SLOTS, :].reshape(AGENTS, D)
        xs[local * LIVE : (local + 1) * LIVE] = dot(gather, x).astype(BF16)

    copies[0].wait()
    for local in range(LOCAL):
        rows = slice(local * LIVE, (local + 1) * LIVE)
        packed[rows] = dot(rms(xs[rows], gains[1:2, :]), qkv_w[...]).astype(BF16)
    for local in range(LOCAL):
        rows = slice(local * LIVE, (local + 1) * LIVE)
        for head in range(D // PAIR):
            low = head * PAIR
            q = packed[rows, low : low + PAIR]
            k = packed[rows, D + low : D + low + PAIR]
            v = packed[rows, 2 * D + low : 2 * D + low + PAIR]
            ctx[rows, low : low + PAIR] = attend(dot_nt(head_split(q), k), v)
    for copy in copies[1:]:
        copy.wait()

    lane = iota((SLOTS, LIVE), 1) - iota((SLOTS, LIVE), 0)
    row = iota((SLOTS, LIVE), 0)
    scatter = jnp.concatenate(
        [
            jnp.where((lane == start) & (row < count), 1.0, 0.0).astype(BF16)
            for start, count in offsets
        ],
        axis=0,
    )
    for local in range(LOCAL):
        rows = slice(local * LIVE, (local + 1) * LIVE)
        o2 = dot(ctx[rows], out_w[...]).astype(BF16)
        x2 = (xs[rows].astype(F32) + o2.astype(F32)).astype(BF16)
        hidden = jnp.maximum(dot(rms(x2, gains[2:3, :]), in_w[...]), 0.0).astype(BF16)
        encoded = (x2.astype(F32) + dot(hidden, back_w[...])).astype(BF16)
        spread = dot(scatter, encoded).astype(BF16)
        result[:, local * SLOTS : (local + 1) * SLOTS, :] = spread.reshape(GROUPS, SLOTS, D)


def scene_part(counts, recv, gains, qkv_w, out_w, mlp_in, mlp_out):
    vmem = pl.BlockSpec(memory_space=pltpu.VMEM)
    hbm = pl.BlockSpec(memory_space=pl.ANY)
    return pl.pallas_call(
        scene_kernel,
        in_specs=[pl.BlockSpec(memory_space=pltpu.SMEM), vmem, vmem, hbm, hbm, hbm, hbm],
        out_specs=vmem,
        out_shape=jax.ShapeDtypeStruct((GROUPS, LOCAL * SLOTS, D), BF16),
        scratch_shapes=[
            pltpu.VMEM((D, 3 * D), BF16),
            pltpu.VMEM((D, D), BF16),
            pltpu.VMEM((D, FF), BF16),
            pltpu.VMEM((FF, D), BF16),
            pltpu.VMEM((LOCAL * LIVE, D), BF16),
            pltpu.VMEM((LOCAL * LIVE, 3 * D), BF16),
            pltpu.VMEM((LOCAL * LIVE, D), BF16),
            pltpu.SemaphoreType.DMA((4,)),
        ],
        compiler_params=pltpu.CompilerParams(vmem_limit_bytes=40 << 20),
        cost_estimate=pl.CostEstimate(
            flops=10 << 30, bytes_accessed=8 << 20, transcendentals=2 << 20
        ),
        name="scene_part",
    )(counts, recv, gains, qkv_w, out_w, mlp_in, mlp_out)


def order_kernel(recv, result):
    rows = recv[...].reshape(256, D)
    result[...] = dot(regroup(), rows).astype(BF16).reshape(SLOTS, 16, D)


def order_part(recv):
    many = 16 // LOCAL
    return pl.pallas_call(
        order_kernel,
        grid=(STEPS // 16,),
        in_specs=[pl.BlockSpec((many, LOCAL * SLOTS, D), lambda i: (i, 0, 0))],
        out_specs=pl.BlockSpec((SLOTS, 16, D), lambda i: (0, i, 0)),
        out_shape=jax.ShapeDtypeStruct((SLOTS, STEPS, D), BF16),
        name="order_part",
    )(recv)


def exchange(values):
    return lax.all_to_all(values, "seq", split_axis=0, concat_axis=0, tiled=True)


def per_device(
    tokens, block_counts, gains, qkv_time, out_time, qkv_scene, out_scene, mlp_in, mlp_out
):
    after_time = exchange(time_part(block_counts, tokens, gains, qkv_time, out_time))
    encoded = scene_part(block_counts, after_time, gains, qkv_scene, out_scene, mlp_in, mlp_out)
    return order_part(exchange(encoded))


def solution(mesh):
    placed = (P(("scene", "seq"), None, None), P("scene"), P(), P(), P(), P(), P(), P(), P())
    return jax.shard_map(
        per_device,
        mesh=mesh,
        in_specs=placed,
        out_specs=P(("scene", "seq"), None, None),
        check_vma=False,
    )
```

```python
import jax
import jax.numpy as jnp
from jax import lax
from jax.experimental import pallas as pl
from jax.experimental.pallas import tpu as pltpu
from jax.sharding import PartitionSpec as P

D = 512
FF = 2048
SLOTS = 16
STEPS = 64
GROUPS = 32
LOCAL = STEPS // GROUPS
AGENTS = SLOTS * GROUPS
LIVE = 320
GROUP = 8
ROWS = GROUP * STEPS
QUAD = 256
LANES = 128
LOWEST = -3e38
INV_ROOT = 0.125
CUTS = 4
BF16 = jnp.bfloat16
F32 = jnp.float32


def dot(a, b):
    return jnp.dot(a, b, preferred_element_type=F32)


def dot_nt(a, b):
    return lax.dot_general(a, b, (((1,), (1,)), ((), ())), preferred_element_type=F32)


def rms(values, gain):
    floats = values.astype(F32)
    inverse = lax.rsqrt(jnp.mean(floats * floats, axis=-1, keepdims=True) + 1e-06)
    return (floats * inverse * gain).astype(BF16)


def iota(shape, dim):
    return lax.broadcasted_iota(jnp.int32, shape, dim)


def regroup():
    row, col = iota((256, 256), 0), iota((256, 256), 1)
    return jnp.where(col == (row & 15) * 16 + (row >> 4), 1.0, 0.0).astype(BF16)


def quad_masks(k):
    lane = iota(k.shape, 1) >> 6
    return jnp.concatenate([jnp.where(lane == h, k, jnp.zeros_like(k)) for h in range(4)], axis=0)


def time_group(values, gains, qkv_w, out_w, ctx):
    packed = dot(rms(values, gains[0:1, :]), qkv_w[...]).astype(BF16)
    ones = quad_masks(jnp.ones((STEPS, QUAD), BF16))
    for agent in range(GROUP):
        rows = slice(agent * STEPS, (agent + 1) * STEPS)
        for low in range(0, D, QUAD):
            q = packed[rows, low : low + QUAD] * jnp.asarray(INV_ROOT, BF16)
            k = packed[rows, D + low : D + low + QUAD]
            v = packed[rows, 2 * D + low : 2 * D + low + QUAD]
            scores = dot_nt(q, quad_masks(k))
            p = []
            for half in range(0, QUAD, LANES):
                part = scores[:, half : half + LANES]
                left = iota(part.shape, 1) < STEPS
                top0 = jnp.max(jnp.where(left, part, LOWEST), axis=-1, keepdims=True)
                top1 = jnp.max(jnp.where(left, LOWEST, part), axis=-1, keepdims=True)
                p.append(jnp.exp(part - jnp.where(left, top0, top1)))
            p = jnp.concatenate(p, axis=1).astype(BF16)
            both = dot(p, jnp.concatenate([quad_masks(v), ones], axis=1))
            ctx[rows, low : low + QUAD] = (both[:, :QUAD] / both[:, QUAD:]).astype(BF16)
    update = dot(ctx[...], out_w[...])
    return (values.astype(F32) + update).astype(BF16)


def scene_quad(q, k, v):
    scores = dot_nt(q * jnp.asarray(INV_ROOT, BF16), quad_masks(k))
    p, inverse = [], []
    for low in range(0, 4 * LIVE, 2 * LIVE):
        a = scores[:, low : low + 256]
        m = scores[:, low + 256 : low + 384]
        b = scores[:, low + 384 : low + 640]
        left = iota(m.shape, 1) < 64
        top0 = jnp.maximum(a[:, :LANES], a[:, LANES:])
        top0 = jnp.max(jnp.maximum(top0, jnp.where(left, m, LOWEST)), axis=-1, keepdims=True)
        top1 = jnp.maximum(b[:, :LANES], b[:, LANES:])
        top1 = jnp.max(jnp.maximum(top1, jnp.where(left, LOWEST, m)), axis=-1, keepdims=True)
        a, b = jnp.exp(a - top0), jnp.exp(b - top1)
        m = jnp.exp(m - jnp.where(left, top0, top1))
        sum0 = a[:, :LANES] + a[:, LANES:] + jnp.where(left, m, 0.0)
        sum1 = b[:, :LANES] + b[:, LANES:] + jnp.where(left, 0.0, m)
        sum0 = jnp.sum(sum0, axis=-1, keepdims=True)
        sum1 = jnp.sum(sum1, axis=-1, keepdims=True)
        p += [a.astype(BF16), m.astype(BF16), b.astype(BF16)]
        inverse.append(1.0 / jnp.where(left, sum0, sum1))
    value = dot(jnp.concatenate(p, axis=1), quad_masks(v))
    return (value * jnp.concatenate(inverse, axis=1)).astype(BF16)


def time_kernel(
    counts, tokens_hbm, gains, qkv_hbm, out_hbm, result, tokens, qkv_w, out_w, x1, ctx, sems
):
    many = SLOTS // GROUP
    cut = D // CUTS

    def tokens_copy(i):
        part = pl.ds(pl.multiple_of(i * GROUP, GROUP), GROUP)
        return pltpu.make_async_copy(tokens_hbm.at[part], tokens.at[part], sems.at[i])

    def weight_copies(source, target, first):
        parts = [pl.ds(i * cut, cut) for i in range(CUTS)]
        return [
            pltpu.make_async_copy(source.at[part], target.at[part], sems.at[first + i])
            for i, part in enumerate(parts)
        ]

    tokens_copy(0).start()
    weights = weight_copies(qkv_hbm, qkv_w, many) + weight_copies(out_hbm, out_w, many + CUTS)
    for copy in weights:
        copy.start()
    for i in range(1, many):
        tokens_copy(i).start()
    count = counts[lax.axis_index("seq")]
    for copy in weights[:CUTS]:
        copy.wait()

    def group(i, _):
        first = pl.multiple_of(i * GROUP, GROUP)
        tokens_copy(i).wait()

        @pl.when(i == 0)
        def _():
            for copy in weights[CUTS:]:
                copy.wait()

        @pl.when(first < count)
        def _():
            values = tokens[pl.ds(first, GROUP)].reshape(ROWS, D)
            after = time_group(values, gains, qkv_w, out_w, ctx)
            x1[pl.ds(first, GROUP)] = after.reshape(GROUP, STEPS, D)

        @pl.when(first >= count)
        def _():
            x1[pl.ds(first, GROUP)] = jnp.zeros((GROUP, STEPS, D), BF16)

        return 0

    lax.fori_loop(0, many, group, 0)
    turn = regroup()
    for part in range(STEPS // 16):
        rows = x1[:, part * 16 : (part + 1) * 16, :].reshape(256, D)
        turned = dot(turn, rows).astype(BF16)
        span = 16 // LOCAL
        result[part * span : (part + 1) * span] = turned.reshape(span, LOCAL * SLOTS, D)


def time_part(counts, tokens, gains, qkv_w, out_w):
    vmem = pl.BlockSpec(memory_space=pltpu.VMEM)
    hbm = pl.BlockSpec(memory_space=pltpu.HBM)
    return pl.pallas_call(
        time_kernel,
        in_specs=[pl.BlockSpec(memory_space=pltpu.SMEM), hbm, vmem, hbm, hbm],
        out_specs=vmem,
        out_shape=jax.ShapeDtypeStruct((GROUPS, LOCAL * SLOTS, D), BF16),
        scratch_shapes=[
            pltpu.VMEM((SLOTS, STEPS, D), BF16),
            pltpu.VMEM((D, 3 * D), BF16),
            pltpu.VMEM((D, D), BF16),
            pltpu.VMEM((SLOTS, STEPS, D), BF16),
            pltpu.VMEM((ROWS, D), BF16),
            pltpu.SemaphoreType.DMA((SLOTS // GROUP + 2 * CUTS,)),
        ],
        compiler_params=pltpu.CompilerParams(vmem_limit_bytes=32 << 20),
        cost_estimate=pl.CostEstimate(
            flops=6 << 30, bytes_accessed=4 << 20, transcendentals=1 << 20
        ),
        name="time_part",
    )(counts, tokens, gains, qkv_w, out_w)


def scene_kernel(
    counts, recv, gains, qkv_w, out_w, in_w, back_w, result, xs, packed, ctx
):
    slot = iota((8, AGENTS), 1)
    inside = slot & 15
    place = jnp.full((8, AGENTS), -1, jnp.int32)
    offsets, offset = [], jnp.int32(0)
    for block in range(GROUPS):
        count = counts[block]
        here = ((slot >> 4) == block) & (inside < count)
        place = jnp.where(here, inside + offset, place)
        offsets.append((offset, count))
        offset = offset + count
    gather = jnp.where(iota((LIVE, AGENTS), 0) == place[0:1], 1.0, 0.0).astype(BF16)
    for local in range(LOCAL):
        x = recv[:, local * SLOTS : (local + 1) * SLOTS, :].reshape(AGENTS, D)
        xs[local * LIVE : (local + 1) * LIVE] = dot(gather, x).astype(BF16)

    blocks = [slice(i * LIVE, (i + 1) * LIVE) for i in range(LOCAL)]
    for rows in blocks:
        packed[rows] = dot(rms(xs[rows], gains[1:2, :]), qkv_w[...]).astype(BF16)
    for rows in blocks:
        for low in range(0, D, QUAD):
            q = packed[rows, low : low + QUAD]
            k = packed[rows, D + low : D + low + QUAD]
            v = packed[rows, 2 * D + low : 2 * D + low + QUAD]
            ctx[rows, low : low + QUAD] = scene_quad(q, k, v)

    lane = iota((SLOTS, LIVE), 1) - iota((SLOTS, LIVE), 0)
    row = iota((SLOTS, LIVE), 0)
    scatter = jnp.concatenate(
        [
            jnp.where((lane == start) & (row < count), 1.0, 0.0).astype(BF16)
            for start, count in offsets
        ],
        axis=0,
    )
    for i, rows in enumerate(blocks):
        o2 = dot(ctx[rows], out_w[...]).astype(BF16)
        x2 = (xs[rows].astype(F32) + o2.astype(F32)).astype(BF16)
        hidden = jnp.maximum(dot(rms(x2, gains[2:3, :]), in_w[...]), 0.0).astype(BF16)
        encoded = (x2.astype(F32) + dot(hidden, back_w[...])).astype(BF16)
        spread = dot(scatter, encoded).astype(BF16)
        result[:, i * SLOTS : (i + 1) * SLOTS, :] = spread.reshape(GROUPS, SLOTS, D)


def scene_part(counts, recv, gains, qkv_w, out_w, mlp_in, mlp_out):
    vmem = pl.BlockSpec(memory_space=pltpu.VMEM)
    return pl.pallas_call(
        scene_kernel,
        in_specs=[pl.BlockSpec(memory_space=pltpu.SMEM)] + [vmem] * 6,
        out_specs=vmem,
        out_shape=jax.ShapeDtypeStruct((GROUPS, LOCAL * SLOTS, D), BF16),
        scratch_shapes=[
            pltpu.VMEM((LOCAL * LIVE, D), BF16),
            pltpu.VMEM((LOCAL * LIVE, 3 * D), BF16),
            pltpu.VMEM((LOCAL * LIVE, D), BF16),
        ],
        compiler_params=pltpu.CompilerParams(vmem_limit_bytes=40 << 20),
        cost_estimate=pl.CostEstimate(
            flops=10 << 30, bytes_accessed=8 << 20, transcendentals=2 << 20
        ),
        name="scene_part",
    )(counts, recv, gains, qkv_w, out_w, mlp_in, mlp_out)


def order_kernel(recv, result, turned, sems):
    turn = regroup()
    span = 16 // LOCAL
    copies = []
    for part in range(STEPS // 16):
        rows = recv[part * span : (part + 1) * span].reshape(256, D)
        turned[part] = dot(turn, rows).astype(BF16).reshape(SLOTS, 16, D)
        copies.append(
            pltpu.make_async_copy(
                turned.at[part], result.at[:, pl.ds(part * 16, 16), :], sems.at[part]
            )
        )
        copies[-1].start()
    for copy in copies:
        copy.wait()


def order_part(recv):
    return pl.pallas_call(
        order_kernel,
        in_specs=[pl.BlockSpec(memory_space=pltpu.VMEM)],
        out_specs=pl.BlockSpec(memory_space=pltpu.HBM),
        out_shape=jax.ShapeDtypeStruct((SLOTS, STEPS, D), BF16),
        scratch_shapes=[
            pltpu.VMEM((STEPS // 16, SLOTS, 16, D), BF16),
            pltpu.SemaphoreType.DMA((STEPS // 16,)),
        ],
        compiler_params=pltpu.CompilerParams(vmem_limit_bytes=16 << 20),
        name="order_part",
    )(recv)


def exchange(values):
    return lax.all_to_all(values, "seq", split_axis=0, concat_axis=0, tiled=True)


def per_device(
    tokens, block_counts, gains, qkv_time, out_time, qkv_scene, out_scene, mlp_in, mlp_out
):
    after_time = exchange(time_part(block_counts, tokens, gains, qkv_time, out_time))
    encoded = scene_part(block_counts, after_time, gains, qkv_scene, out_scene, mlp_in, mlp_out)
    return order_part(exchange(encoded))


def solution(mesh):
    placed = (P(("scene", "seq"), None, None), P("scene"), P(), P(), P(), P(), P(), P(), P())
    return jax.shard_map(
        per_device,
        mesh=mesh,
        in_specs=placed,
        out_specs=P(("scene", "seq"), None, None),
        check_vma=False,
    )
```

```python
import jax
import jax.numpy as jnp
from jax import lax
from jax.experimental import pallas as pl
from jax.experimental.pallas import tpu as pltpu
from jax.sharding import PartitionSpec as P

D = 512
FF = 2048
SLOTS = 16
STEPS = 64
GROUPS = 32
LOCAL = STEPS // GROUPS
AGENTS = SLOTS * GROUPS
LIVE = 320
GROUP = 8
ROWS = GROUP * STEPS
QUAD = 256
LANES = 128
LOWEST = -3e38
INV_ROOT = 0.125
CUTS = 4
BF16 = jnp.bfloat16
F32 = jnp.float32


def dot(a, b):
    return jnp.dot(a, b, preferred_element_type=F32)


def dot_nt(a, b):
    return lax.dot_general(a, b, (((1,), (1,)), ((), ())), preferred_element_type=F32)


def rms(values, gain):
    floats = values.astype(F32)
    inverse = lax.rsqrt(jnp.mean(floats * floats, axis=-1, keepdims=True) + 1e-06)
    return (floats * inverse * gain).astype(BF16)


def iota(shape, dim):
    return lax.broadcasted_iota(jnp.int32, shape, dim)


def regroup():
    row, col = iota((256, 256), 0), iota((256, 256), 1)
    return jnp.where(col == (row & 15) * 16 + (row >> 4), 1.0, 0.0).astype(BF16)


def quad_masks(k):
    lane = iota(k.shape, 1) >> 6
    return jnp.concatenate([jnp.where(lane == h, k, jnp.zeros_like(k)) for h in range(4)], axis=0)


def time_group(values, gains, qkv_w, out_w, ctx):
    packed = dot(rms(values, gains[0:1, :]), qkv_w[...]).astype(BF16)
    ones = quad_masks(jnp.ones((STEPS, QUAD), BF16))
    for agent in range(GROUP):
        rows = slice(agent * STEPS, (agent + 1) * STEPS)
        for low in range(0, D, QUAD):
            q = packed[rows, low : low + QUAD] * jnp.asarray(INV_ROOT, BF16)
            k = packed[rows, D + low : D + low + QUAD]
            v = packed[rows, 2 * D + low : 2 * D + low + QUAD]
            scores = dot_nt(q, quad_masks(k))
            p = []
            for half in range(0, QUAD, LANES):
                part = scores[:, half : half + LANES]
                left = iota(part.shape, 1) < STEPS
                top0 = jnp.max(jnp.where(left, part, LOWEST), axis=-1, keepdims=True)
                top1 = jnp.max(jnp.where(left, LOWEST, part), axis=-1, keepdims=True)
                p.append(jnp.exp(part - jnp.where(left, top0, top1)))
            p = jnp.concatenate(p, axis=1).astype(BF16)
            both = dot(p, jnp.concatenate([quad_masks(v), ones], axis=1))
            ctx[rows, low : low + QUAD] = (both[:, :QUAD] / both[:, QUAD:]).astype(BF16)
    update = dot(ctx[...], out_w[...])
    return (values.astype(F32) + update).astype(BF16)


def scene_quad(q, k, v):
    scores = dot_nt(q * jnp.asarray(INV_ROOT, BF16), quad_masks(k))
    p, inverse = [], []
    for low in range(0, 4 * LIVE, 2 * LIVE):
        a = scores[:, low : low + 256]
        m = scores[:, low + 256 : low + 384]
        b = scores[:, low + 384 : low + 640]
        left = iota(m.shape, 1) < 64
        top0 = jnp.maximum(a[:, :LANES], a[:, LANES:])
        top0 = jnp.max(jnp.maximum(top0, jnp.where(left, m, LOWEST)), axis=-1, keepdims=True)
        top1 = jnp.maximum(b[:, :LANES], b[:, LANES:])
        top1 = jnp.max(jnp.maximum(top1, jnp.where(left, LOWEST, m)), axis=-1, keepdims=True)
        a, b = jnp.exp(a - top0), jnp.exp(b - top1)
        m = jnp.exp(m - jnp.where(left, top0, top1))
        sum0 = a[:, :LANES] + a[:, LANES:] + jnp.where(left, m, 0.0)
        sum1 = b[:, :LANES] + b[:, LANES:] + jnp.where(left, 0.0, m)
        sum0 = jnp.sum(sum0, axis=-1, keepdims=True)
        sum1 = jnp.sum(sum1, axis=-1, keepdims=True)
        p += [a.astype(BF16), m.astype(BF16), b.astype(BF16)]
        inverse.append(1.0 / jnp.where(left, sum0, sum1))
    value = dot(jnp.concatenate(p, axis=1), quad_masks(v))
    return (value * jnp.concatenate(inverse, axis=1)).astype(BF16)


def time_kernel(
    counts, tokens_hbm, gains, qkv_hbm, out_hbm, result, tokens, qkv_w, out_w, x1, ctx, sems
):
    many = SLOTS // GROUP
    cut = D // CUTS

    def tokens_copy(i):
        part = pl.ds(pl.multiple_of(i * GROUP, GROUP), GROUP)
        return pltpu.make_async_copy(tokens_hbm.at[part], tokens.at[part], sems.at[i])

    def weight_copies(source, target, first):
        parts = [pl.ds(i * cut, cut) for i in range(CUTS)]
        return [
            pltpu.make_async_copy(source.at[part], target.at[part], sems.at[first + i])
            for i, part in enumerate(parts)
        ]

    tokens_copy(0).start()
    weights = weight_copies(qkv_hbm, qkv_w, many) + weight_copies(out_hbm, out_w, many + CUTS)
    for copy in weights:
        copy.start()
    for i in range(1, many):
        tokens_copy(i).start()
    count = counts[lax.axis_index("seq")]
    for copy in weights[:CUTS]:
        copy.wait()

    def group(i, _):
        first = pl.multiple_of(i * GROUP, GROUP)
        tokens_copy(i).wait()

        @pl.when(i == 0)
        def _():
            for copy in weights[CUTS:]:
                copy.wait()

        @pl.when(first < count)
        def _():
            values = tokens[pl.ds(first, GROUP)].reshape(ROWS, D)
            after = time_group(values, gains, qkv_w, out_w, ctx)
            x1[pl.ds(first, GROUP)] = after.reshape(GROUP, STEPS, D)

        @pl.when(first >= count)
        def _():
            x1[pl.ds(first, GROUP)] = jnp.zeros((GROUP, STEPS, D), BF16)

        return 0

    lax.fori_loop(0, many, group, 0)
    turn = regroup()
    for part in range(STEPS // 16):
        rows = x1[:, part * 16 : (part + 1) * 16, :].reshape(256, D)
        turned = dot(turn, rows).astype(BF16)
        span = 16 // LOCAL
        result[part * span : (part + 1) * span] = turned.reshape(span, LOCAL * SLOTS, D)


def time_part(counts, tokens, gains, qkv_w, out_w):
    vmem = pl.BlockSpec(memory_space=pltpu.VMEM)
    hbm = pl.BlockSpec(memory_space=pltpu.HBM)
    return pl.pallas_call(
        time_kernel,
        in_specs=[pl.BlockSpec(memory_space=pltpu.SMEM), hbm, vmem, hbm, hbm],
        out_specs=vmem,
        out_shape=jax.ShapeDtypeStruct((GROUPS, LOCAL * SLOTS, D), BF16),
        scratch_shapes=[
            pltpu.VMEM((SLOTS, STEPS, D), BF16),
            pltpu.VMEM((D, 3 * D), BF16),
            pltpu.VMEM((D, D), BF16),
            pltpu.VMEM((SLOTS, STEPS, D), BF16),
            pltpu.VMEM((ROWS, D), BF16),
            pltpu.SemaphoreType.DMA((SLOTS // GROUP + 2 * CUTS,)),
        ],
        compiler_params=pltpu.CompilerParams(vmem_limit_bytes=32 << 20),
        cost_estimate=pl.CostEstimate(
            flops=6 << 30, bytes_accessed=4 << 20, transcendentals=1 << 20
        ),
        name="time_part",
    )(*(pltpu.with_memory_space_constraint(x, pltpu.HBM) for x in (counts, tokens, gains, qkv_w, out_w)))


def scene_kernel(
    counts, recv, gains, qkv_w, out_w, in_w, back_w, result, xs, packed, ctx
):
    slot = iota((8, AGENTS), 1)
    inside = slot & 15
    place = jnp.full((8, AGENTS), -1, jnp.int32)
    offsets, offset = [], jnp.int32(0)
    for block in range(GROUPS):
        count = counts[block]
        here = ((slot >> 4) == block) & (inside < count)
        place = jnp.where(here, inside + offset, place)
        offsets.append((offset, count))
        offset = offset + count
    gather = jnp.where(iota((LIVE, AGENTS), 0) == place[0:1], 1.0, 0.0).astype(BF16)
    for local in range(LOCAL):
        x = recv[:, local * SLOTS : (local + 1) * SLOTS, :].reshape(AGENTS, D)
        xs[local * LIVE : (local + 1) * LIVE] = dot(gather, x).astype(BF16)

    blocks = [slice(i * LIVE, (i + 1) * LIVE) for i in range(LOCAL)]
    for rows in blocks:
        packed[rows] = dot(rms(xs[rows], gains[1:2, :]), qkv_w[...]).astype(BF16)
    for rows in blocks:
        for low in range(0, D, QUAD):
            q = packed[rows, low : low + QUAD]
            k = packed[rows, D + low : D + low + QUAD]
            v = packed[rows, 2 * D + low : 2 * D + low + QUAD]
            ctx[rows, low : low + QUAD] = scene_quad(q, k, v)

    lane = iota((SLOTS, LIVE), 1) - iota((SLOTS, LIVE), 0)
    row = iota((SLOTS, LIVE), 0)
    scatter = jnp.concatenate(
        [
            jnp.where((lane == start) & (row < count), 1.0, 0.0).astype(BF16)
            for start, count in offsets
        ],
        axis=0,
    )
    for i, rows in enumerate(blocks):
        o2 = dot(ctx[rows], out_w[...]).astype(BF16)
        x2 = (xs[rows].astype(F32) + o2.astype(F32)).astype(BF16)
        hidden = jnp.maximum(dot(rms(x2, gains[2:3, :]), in_w[...]), 0.0).astype(BF16)
        encoded = (x2.astype(F32) + dot(hidden, back_w[...])).astype(BF16)
        spread = dot(scatter, encoded).astype(BF16)
        result[:, i * SLOTS : (i + 1) * SLOTS, :] = spread.reshape(GROUPS, SLOTS, D)


def scene_part(counts, recv, gains, qkv_w, out_w, mlp_in, mlp_out):
    vmem = pl.BlockSpec(memory_space=pltpu.VMEM)
    return pl.pallas_call(
        scene_kernel,
        in_specs=[pl.BlockSpec(memory_space=pltpu.SMEM)] + [vmem] * 6,
        out_specs=vmem,
        out_shape=jax.ShapeDtypeStruct((GROUPS, LOCAL * SLOTS, D), BF16),
        scratch_shapes=[
            pltpu.VMEM((LOCAL * LIVE, D), BF16),
            pltpu.VMEM((LOCAL * LIVE, 3 * D), BF16),
            pltpu.VMEM((LOCAL * LIVE, D), BF16),
        ],
        compiler_params=pltpu.CompilerParams(vmem_limit_bytes=40 << 20),
        cost_estimate=pl.CostEstimate(
            flops=10 << 30, bytes_accessed=8 << 20, transcendentals=2 << 20
        ),
        name="scene_part",
    )(counts, recv, gains, qkv_w, out_w, mlp_in, mlp_out)


def order_kernel(recv, result, turned, sems):
    turn = regroup()
    span = 16 // LOCAL
    copies = []
    for part in range(STEPS // 16):
        rows = recv[part * span : (part + 1) * span].reshape(256, D)
        turned[part] = dot(turn, rows).astype(BF16).reshape(SLOTS, 16, D)
        copies.append(
            pltpu.make_async_copy(
                turned.at[part], result.at[:, pl.ds(part * 16, 16), :], sems.at[part]
            )
        )
        copies[-1].start()
    for copy in copies:
        copy.wait()


def order_part(recv):
    return pl.pallas_call(
        order_kernel,
        in_specs=[pl.BlockSpec(memory_space=pltpu.VMEM)],
        out_specs=pl.BlockSpec(memory_space=pltpu.HBM),
        out_shape=jax.ShapeDtypeStruct((SLOTS, STEPS, D), BF16),
        scratch_shapes=[
            pltpu.VMEM((STEPS // 16, SLOTS, 16, D), BF16),
            pltpu.SemaphoreType.DMA((STEPS // 16,)),
        ],
        compiler_params=pltpu.CompilerParams(vmem_limit_bytes=16 << 20),
        name="order_part",
    )(recv)


def exchange(values):
    return lax.all_to_all(values, "seq", split_axis=0, concat_axis=0, tiled=True)


def per_device(
    tokens, block_counts, gains, qkv_time, out_time, qkv_scene, out_scene, mlp_in, mlp_out
):
    after_time = time_part(block_counts, tokens, gains, qkv_time, out_time)
    after_time, *rest = lax.optimization_barrier(
        (after_time, block_counts, gains, qkv_scene, out_scene, mlp_in, mlp_out)
    )
    counts, *rest = rest
    encoded = scene_part(counts, exchange(after_time), *rest)
    return order_part(exchange(encoded))


def solution(mesh):
    placed = (P(("scene", "seq"), None, None), P("scene"), P(), P(), P(), P(), P(), P(), P())
    return jax.shard_map(
        per_device,
        mesh=mesh,
        in_specs=placed,
        out_specs=P(("scene", "seq"), None, None),
        check_vma=False,
    )
```

```python
import functools

import jax
import jax.numpy as jnp
from jax import lax
from jax.experimental import pallas as pl
from jax.experimental.pallas import tpu as pltpu
from jax.sharding import PartitionSpec as P

D = 512
FF = 2048
SLOTS = 16
STEPS = 64
GROUPS = 32
LOCAL = STEPS // GROUPS
AGENTS = SLOTS * GROUPS
LIVE = 320
QUAD = 256
LANES = 128
LOWEST = -3e38
INV_ROOT = 0.125
EARLY = 4
LATE_SIZE = 4
CUTS = 4
BF16 = jnp.bfloat16
F32 = jnp.float32


def dot(a, b):
    return jnp.dot(a, b, preferred_element_type=F32)


def dot_nt(a, b):
    return lax.dot_general(a, b, (((1,), (1,)), ((), ())), preferred_element_type=F32)


def rms(values, gain):
    floats = values.astype(F32)
    inverse = lax.rsqrt(jnp.mean(floats * floats, axis=-1, keepdims=True) + 1e-06)
    return (floats * inverse * gain).astype(BF16)


def iota(shape, dim):
    return lax.broadcasted_iota(jnp.int32, shape, dim)


def regroup(slots):
    size = (slots * 16, slots * 16)
    row, col = iota(size, 0), iota(size, 1)
    return jnp.where(row == (col & 15) * slots + (col >> 4), 1.0, 0.0).astype(BF16)


def quad_masks(k):
    lane = iota(k.shape, 1) >> 6
    return jnp.concatenate([jnp.where(lane == h, k, jnp.zeros_like(k)) for h in range(4)], axis=0)


def time_group(values, gains, qkv_w, out_w, ctx):
    agents = values.shape[0] // STEPS
    packed = dot(rms(values, gains[0:1, :]), qkv_w[...]).astype(BF16)
    ones = quad_masks(jnp.ones((STEPS, QUAD), BF16))
    for agent in range(agents):
        rows = slice(agent * STEPS, (agent + 1) * STEPS)
        for low in range(0, D, QUAD):
            q = packed[rows, low : low + QUAD] * jnp.asarray(INV_ROOT, BF16)
            k = packed[rows, D + low : D + low + QUAD]
            v = packed[rows, 2 * D + low : 2 * D + low + QUAD]
            scores = dot_nt(q, quad_masks(k))
            p = []
            for half in range(0, QUAD, LANES):
                part = scores[:, half : half + LANES]
                left = iota(part.shape, 1) < STEPS
                top0 = jnp.max(jnp.where(left, part, LOWEST), axis=-1, keepdims=True)
                top1 = jnp.max(jnp.where(left, LOWEST, part), axis=-1, keepdims=True)
                p.append(jnp.exp(part - jnp.where(left, top0, top1)))
            p = jnp.concatenate(p, axis=1).astype(BF16)
            both = dot(p, jnp.concatenate([quad_masks(v), ones], axis=1))
            ctx[rows, low : low + QUAD] = (both[:, :QUAD] / both[:, QUAD:]).astype(BF16)
    update = dot(ctx[...], out_w[...])
    return (values.astype(F32) + update).astype(BF16)


def scene_quad(q, k, v):
    scores = dot_nt(q * jnp.asarray(INV_ROOT, BF16), quad_masks(k))
    p, inverse = [], []
    for low in range(0, 4 * LIVE, 2 * LIVE):
        a = scores[:, low : low + 256]
        m = scores[:, low + 256 : low + 384]
        b = scores[:, low + 384 : low + 640]
        left = iota(m.shape, 1) < 64
        top0 = jnp.maximum(a[:, :LANES], a[:, LANES:])
        top0 = jnp.max(jnp.maximum(top0, jnp.where(left, m, LOWEST)), axis=-1, keepdims=True)
        top1 = jnp.maximum(b[:, :LANES], b[:, LANES:])
        top1 = jnp.max(jnp.maximum(top1, jnp.where(left, LOWEST, m)), axis=-1, keepdims=True)
        a, b = jnp.exp(a - top0), jnp.exp(b - top1)
        m = jnp.exp(m - jnp.where(left, top0, top1))
        sum0 = a[:, :LANES] + a[:, LANES:] + jnp.where(left, m, 0.0)
        sum1 = b[:, :LANES] + b[:, LANES:] + jnp.where(left, 0.0, m)
        sum0 = jnp.sum(sum0, axis=-1, keepdims=True)
        sum1 = jnp.sum(sum1, axis=-1, keepdims=True)
        p += [a.astype(BF16), m.astype(BF16), b.astype(BF16)]
        inverse.append(1.0 / jnp.where(left, sum0, sum1))
    value = dot(jnp.concatenate(p, axis=1), quad_masks(v))
    return (value * jnp.concatenate(inverse, axis=1)).astype(BF16)


def time_kernel(base, size, extra, counts, tokens_hbm, gains, qkv_hbm, out_hbm, *refs):
    later_hbm, (result, *later) = refs[:extra], refs[extra : 2 * extra + 1]
    tokens, qkv_w, out_w, x1, ctx, sems, later_sems = refs[2 * extra + 1 :]
    slots = tokens.shape[0]
    many = slots // size
    cut = D // CUTS

    def tokens_copy(i):
        first = pl.multiple_of(i * size, size)
        source = tokens_hbm.at[pl.ds(base + first, size)]
        return pltpu.make_async_copy(source, tokens.at[pl.ds(first, size)], sems.at[i])

    def weight_copies(source, target, first):
        parts = [pl.ds(i * cut, cut) for i in range(CUTS)]
        return [
            pltpu.make_async_copy(source.at[part], target.at[part], sems.at[first + i])
            for i, part in enumerate(parts)
        ]

    tokens_copy(0).start()
    weights = weight_copies(qkv_hbm, qkv_w, many) + weight_copies(out_hbm, out_w, many + CUTS)
    for copy in weights:
        copy.start()
    for i in range(1, many):
        tokens_copy(i).start()
    count = counts[lax.axis_index("seq")]
    for copy in weights[:CUTS]:
        copy.wait()
    fetches = [
        pltpu.make_async_copy(source, target, later_sems.at[i])
        for i, (source, target) in enumerate(zip(later_hbm, later))
    ]
    for fetch in fetches:
        fetch.start()

    def group(i, _):
        first = pl.multiple_of(i * size, size)
        tokens_copy(i).wait()

        @pl.when(i == 0)
        def _():
            for copy in weights[CUTS:]:
                copy.wait()

        @pl.when(base + first < count)
        def _():
            values = tokens[pl.ds(first, size)].reshape(size * STEPS, D)
            after = time_group(values, gains, qkv_w, out_w, ctx)
            x1[pl.ds(first, size)] = after.reshape(size, STEPS, D)

        @pl.when(base + first >= count)
        def _():
            x1[pl.ds(first, size)] = jnp.zeros((size, STEPS, D), BF16)

        return 0

    lax.fori_loop(0, many, group, 0)
    turn = regroup(slots)
    for part in range(STEPS // 16):
        rows = x1[:, part * 16 : (part + 1) * 16, :].reshape(slots * 16, D)
        turned = dot(turn, rows).astype(BF16)
        span = 16 // LOCAL
        result[part * span : (part + 1) * span] = turned.reshape(span, LOCAL * slots, D)
    for fetch in fetches:
        fetch.wait()


def time_part(base, slots, size, arrays, later=()):
    vmem = pl.BlockSpec(memory_space=pltpu.VMEM)
    hbm = pl.BlockSpec(memory_space=pltpu.HBM)
    extra = len(later)
    shapes = [jax.ShapeDtypeStruct((GROUPS, LOCAL * slots, D), BF16)]
    result, *fetched = pl.pallas_call(
        functools.partial(time_kernel, base, size, extra),
        in_specs=[pl.BlockSpec(memory_space=pltpu.SMEM), hbm, vmem, hbm, hbm] + [hbm] * extra,
        out_specs=[vmem] * (1 + extra),
        out_shape=shapes + [jax.ShapeDtypeStruct(x.shape, x.dtype) for x in later],
        scratch_shapes=[
            pltpu.VMEM((slots, STEPS, D), BF16),
            pltpu.VMEM((D, 3 * D), BF16),
            pltpu.VMEM((D, D), BF16),
            pltpu.VMEM((slots, STEPS, D), BF16),
            pltpu.VMEM((size * STEPS, D), BF16),
            pltpu.SemaphoreType.DMA((slots // size + 2 * CUTS,)),
            pltpu.SemaphoreType.DMA((max(extra, 1),)),
        ],
        compiler_params=pltpu.CompilerParams(vmem_limit_bytes=32 << 20),
        cost_estimate=pl.CostEstimate(
            flops=slots * (6 << 26), bytes_accessed=4 << 20, transcendentals=slots << 16
        ),
        name=f"time_part_{base}_{slots}",
    )(*(pltpu.with_memory_space_constraint(x, pltpu.HBM) for x in (*arrays, *later)))
    return result, fetched


def scene_kernel(parts, fetch, counts, *refs):
    many = len(parts)
    recv, (gains, *weights, result, xs, packed, ctx) = refs[:many], refs[many:][:9]
    copies = []
    if fetch:
        *targets, sems = refs[many + 9 :]
        sources, weights = weights[-fetch:], weights[:-fetch] + targets
        copies = [
            pltpu.make_async_copy(source, target, sems.at[i])
            for i, (source, target) in enumerate(zip(sources, targets))
        ]
    for copy in copies:
        copy.start()
    qkv_w, out_w, in_w, back_w = weights
    offsets, offset = [], jnp.int32(0)
    for block in range(GROUPS):
        offsets.append((offset, counts[block]))
        offset = offset + counts[block]

    def places(block_of, slot):
        start, count = jnp.zeros_like(block_of), jnp.zeros_like(block_of)
        for block, (first, live) in enumerate(offsets):
            mine = block_of == block
            start = jnp.where(mine, first, start)
            count = jnp.where(mine, live, count)
        return jnp.where(slot < count, slot + start, -1)

    def gather(place):
        return jnp.where(iota((LIVE, place.shape[1]), 0) == place[0:1], 1.0, 0.0).astype(BF16)

    if many == 1:
        column = iota((8, AGENTS), 1)
        whole = gather(places(column >> 4, column & 15))
        for local in range(LOCAL):
            x = recv[0][:, local * SLOTS : (local + 1) * SLOTS, :].reshape(AGENTS, D)
            xs[local * LIVE : (local + 1) * LIVE] = dot(whole, x).astype(BF16)
    else:
        placed = []
        for base, slots in parts:
            width = LOCAL * slots
            column = iota((8, GROUPS * width), 1)
            block_of = (column * (65536 // width + 1)) >> 16
            row = column - block_of * width
            local_of = jnp.where(row < slots, 0, 1)
            place = places(block_of, base + row - local_of * slots)
            placed.append((place, local_of))
        for local in range(LOCAL):
            x = 0.0
            for ref, (place, local_of) in zip(recv, placed):
                pick = gather(jnp.where(local_of == local, place, -1))
                x = x + dot(pick, ref[...].reshape(pick.shape[1], D))
            xs[local * LIVE : (local + 1) * LIVE] = x.astype(BF16)

    blocks = [slice(i * LIVE, (i + 1) * LIVE) for i in range(LOCAL)]
    for rows in blocks:
        packed[rows] = dot(rms(xs[rows], gains[1:2, :]), qkv_w[...]).astype(BF16)
    for rows in blocks:
        for low in range(0, D, QUAD):
            q = packed[rows, low : low + QUAD]
            k = packed[rows, D + low : D + low + QUAD]
            v = packed[rows, 2 * D + low : 2 * D + low + QUAD]
            ctx[rows, low : low + QUAD] = scene_quad(q, k, v)

    for copy in copies:
        copy.wait()
    lane = iota((SLOTS, LIVE), 1) - iota((SLOTS, LIVE), 0)
    row = iota((SLOTS, LIVE), 0)
    scatter = jnp.concatenate(
        [
            jnp.where((lane == start) & (row < count), 1.0, 0.0).astype(BF16)
            for start, count in offsets
        ],
        axis=0,
    )
    for i, rows in enumerate(blocks):
        o2 = dot(ctx[rows], out_w[...]).astype(BF16)
        x2 = (xs[rows].astype(F32) + o2.astype(F32)).astype(BF16)
        hidden = jnp.maximum(dot(rms(x2, gains[2:3, :]), in_w[...]), 0.0).astype(BF16)
        encoded = (x2.astype(F32) + dot(hidden, back_w[...])).astype(BF16)
        spread = dot(scatter, encoded).astype(BF16)
        result[:, i * SLOTS : (i + 1) * SLOTS, :] = spread.reshape(GROUPS, SLOTS, D)


def scene_part(parts, recv, counts, gains, weights, fetch):
    vmem = pl.BlockSpec(memory_space=pltpu.VMEM)
    hbm = pl.BlockSpec(memory_space=pltpu.HBM)
    scratch = [
        pltpu.VMEM((LOCAL * LIVE, D), BF16),
        pltpu.VMEM((LOCAL * LIVE, 3 * D), BF16),
        pltpu.VMEM((LOCAL * LIVE, D), BF16),
    ]
    weights, later = list(weights[: 4 - fetch]), weights[4 - fetch :]
    for x in later:
        weights.append(pltpu.with_memory_space_constraint(x, pltpu.HBM))
        scratch.append(pltpu.VMEM(x.shape, x.dtype))
    if fetch:
        scratch.append(pltpu.SemaphoreType.DMA((fetch,)))
    specs = [pl.BlockSpec(memory_space=pltpu.SMEM)] + [vmem] * (len(recv) + 5 - fetch)
    return pl.pallas_call(
        functools.partial(scene_kernel, parts, fetch),
        in_specs=specs + [hbm] * fetch,
        out_specs=vmem,
        out_shape=jax.ShapeDtypeStruct((GROUPS, LOCAL * SLOTS, D), BF16),
        scratch_shapes=scratch,
        compiler_params=pltpu.CompilerParams(vmem_limit_bytes=40 << 20),
        cost_estimate=pl.CostEstimate(
            flops=10 << 30, bytes_accessed=8 << 20, transcendentals=2 << 20
        ),
        name=f"scene_part_{len(parts)}",
    )(counts, *recv, gains, *weights)


def order_kernel(recv, result, turned, sems):
    turn = regroup(SLOTS)
    span = 16 // LOCAL
    copies = []
    for part in range(STEPS // 16):
        rows = recv[part * span : (part + 1) * span].reshape(256, D)
        turned[part] = dot(turn, rows).astype(BF16).reshape(SLOTS, 16, D)
        copies.append(
            pltpu.make_async_copy(
                turned.at[part], result.at[:, pl.ds(part * 16, 16), :], sems.at[part]
            )
        )
        copies[-1].start()
    for copy in copies:
        copy.wait()


def order_part(recv):
    return pl.pallas_call(
        order_kernel,
        in_specs=[pl.BlockSpec(memory_space=pltpu.VMEM)],
        out_specs=pl.BlockSpec(memory_space=pltpu.HBM),
        out_shape=jax.ShapeDtypeStruct((SLOTS, STEPS, D), BF16),
        scratch_shapes=[
            pltpu.VMEM((STEPS // 16, SLOTS, 16, D), BF16),
            pltpu.SemaphoreType.DMA((STEPS // 16,)),
        ],
        compiler_params=pltpu.CompilerParams(vmem_limit_bytes=16 << 20),
        name="order_part",
    )(recv)


def exchange(values):
    return lax.all_to_all(values, "seq", split_axis=0, concat_axis=0, tiled=True)


def one_exchange(counts, tokens, gains, qkv_time, out_time, *weights):
    arrays = (counts, tokens, gains, qkv_time, out_time)
    after_time, fetched = time_part(0, SLOTS, 8, arrays, weights)
    recv = [exchange(after_time)]
    return exchange(scene_part([(0, SLOTS)], recv, counts, gains, fetched, 0))


def two_exchanges(counts, tokens, gains, qkv_time, out_time, *weights):
    arrays = (counts, tokens, gains, qkv_time, out_time)
    parts = [(0, EARLY), (EARLY, SLOTS - EARLY)]
    early, _ = time_part(*parts[0], EARLY, arrays)
    late, fetched = time_part(*parts[1], LATE_SIZE, arrays, weights[:2])
    recv = [exchange(early), exchange(late)]
    return exchange(scene_part(parts, recv, counts, gains, (*fetched, *weights[2:]), 2))


def per_device(
    tokens, block_counts, gains, qkv_time, out_time, qkv_scene, out_scene, mlp_in, mlp_out
):
    returned = lax.cond(
        lax.axis_index("scene") % 2 == 0,
        one_exchange,
        two_exchanges,
        block_counts, tokens, gains, qkv_time, out_time, qkv_scene, out_scene, mlp_in, mlp_out,
    )
    return order_part(returned)


def solution(mesh):
    placed = (P(("scene", "seq"), None, None), P("scene"), P(), P(), P(), P(), P(), P(), P())
    return jax.shard_map(
        per_device,
        mesh=mesh,
        in_specs=placed,
        out_specs=P(("scene", "seq"), None, None),
        check_vma=False,
    )
```

```python
import functools

import jax
import jax.numpy as jnp
from jax import lax
from jax.experimental import pallas as pl
from jax.experimental.pallas import tpu as pltpu
from jax.sharding import PartitionSpec as P

D = 512
FF = 2048
SLOTS = 16
STEPS = 64
GROUPS = 32
LOCAL = STEPS // GROUPS
AGENTS = SLOTS * GROUPS
LIVE = 320
QUAD = 256
LANES = 128
LOWEST = -3e38
INV_ROOT = 0.125
EARLY = 4
LATE_SIZE = 4
KEEP = False
CUTS = 4
BF16 = jnp.bfloat16
F32 = jnp.float32


def dot(a, b):
    return jnp.dot(a, b, preferred_element_type=F32)


def dot_nt(a, b):
    return lax.dot_general(a, b, (((1,), (1,)), ((), ())), preferred_element_type=F32)


def rms(values, gain):
    floats = values.astype(F32)
    inverse = lax.rsqrt(jnp.mean(floats * floats, axis=-1, keepdims=True) + 1e-06)
    return (floats * inverse * gain).astype(BF16)


def iota(shape, dim):
    return lax.broadcasted_iota(jnp.int32, shape, dim)


def regroup(slots):
    size = (slots * 16, slots * 16)
    row, col = iota(size, 0), iota(size, 1)
    return jnp.where(row == (col & 15) * slots + (col >> 4), 1.0, 0.0).astype(BF16)


def quad_masks(k):
    lane = iota(k.shape, 1) >> 6
    return jnp.concatenate([jnp.where(lane == h, k, jnp.zeros_like(k)) for h in range(4)], axis=0)


def time_group(values, normed, qkv_w, out_w, ctx):
    agents = values.shape[0] // STEPS
    packed = dot(normed, qkv_w[...]).astype(BF16)
    ones = quad_masks(jnp.ones((STEPS, QUAD), BF16))
    for agent in range(agents):
        rows = slice(agent * STEPS, (agent + 1) * STEPS)
        for low in range(0, D, QUAD):
            q = packed[rows, low : low + QUAD] * jnp.asarray(INV_ROOT, BF16)
            k = packed[rows, D + low : D + low + QUAD]
            v = packed[rows, 2 * D + low : 2 * D + low + QUAD]
            scores = dot_nt(q, quad_masks(k))
            p = []
            for half in range(0, QUAD, LANES):
                part = scores[:, half : half + LANES]
                left = iota(part.shape, 1) < STEPS
                top0 = jnp.max(jnp.where(left, part, LOWEST), axis=-1, keepdims=True)
                top1 = jnp.max(jnp.where(left, LOWEST, part), axis=-1, keepdims=True)
                p.append(jnp.exp(part - jnp.where(left, top0, top1)))
            p = jnp.concatenate(p, axis=1).astype(BF16)
            both = dot(p, jnp.concatenate([quad_masks(v), ones], axis=1))
            ctx[rows, low : low + QUAD] = (both[:, :QUAD] / both[:, QUAD:]).astype(BF16)
    update = dot(ctx[...], out_w[...])
    return (values.astype(F32) + update).astype(BF16)


def scene_quad(q, k, v):
    scores = dot_nt(q * jnp.asarray(INV_ROOT, BF16), quad_masks(k))
    p, inverse = [], []
    for low in range(0, 4 * LIVE, 2 * LIVE):
        a = scores[:, low : low + 256]
        m = scores[:, low + 256 : low + 384]
        b = scores[:, low + 384 : low + 640]
        left = iota(m.shape, 1) < 64
        top0 = jnp.maximum(a[:, :LANES], a[:, LANES:])
        top0 = jnp.max(jnp.maximum(top0, jnp.where(left, m, LOWEST)), axis=-1, keepdims=True)
        top1 = jnp.maximum(b[:, :LANES], b[:, LANES:])
        top1 = jnp.max(jnp.maximum(top1, jnp.where(left, LOWEST, m)), axis=-1, keepdims=True)
        a, b = jnp.exp(a - top0), jnp.exp(b - top1)
        m = jnp.exp(m - jnp.where(left, top0, top1))
        sum0 = a[:, :LANES] + a[:, LANES:] + jnp.where(left, m, 0.0)
        sum1 = b[:, :LANES] + b[:, LANES:] + jnp.where(left, 0.0, m)
        sum0 = jnp.sum(sum0, axis=-1, keepdims=True)
        sum1 = jnp.sum(sum1, axis=-1, keepdims=True)
        p += [a.astype(BF16), m.astype(BF16), b.astype(BF16)]
        inverse.append(1.0 / jnp.where(left, sum0, sum1))
    value = dot(jnp.concatenate(p, axis=1), quad_masks(v))
    return (value * jnp.concatenate(inverse, axis=1)).astype(BF16)


def time_kernel(base, size, own, keep, extra, counts_hbm, tokens_hbm, gains_hbm, *refs):
    refs = list(refs)
    take = lambda many: [refs.pop(0) for _ in range(many)]
    sources, later_hbm, (result,) = take(2), take(extra), take(1)
    kept, later, (counts, gains, tokens) = take(2 * keep), take(extra), take(3)
    weights = (kept or take(2)) if own else sources
    x1, ctx, sems, token_sems, weight_sems, later_sems = refs
    slots = tokens.shape[0]
    many = slots // size
    cut = D // CUTS
    small = [
        pltpu.make_async_copy(counts_hbm, counts, sems.at[0]),
        pltpu.make_async_copy(gains_hbm, gains, sems.at[1]),
    ]

    def tokens_copy(i):
        first = pl.multiple_of(i * size, size)
        source = tokens_hbm.at[pl.ds(base + first, size)]
        return pltpu.make_async_copy(source, tokens.at[pl.ds(first, size)], token_sems.at[i])

    weight_copies = [
        pltpu.make_async_copy(
            sources[w].at[pl.ds(i * cut, cut)],
            weights[w].at[pl.ds(i * cut, cut)],
            weight_sems.at[w * CUTS + i],
        )
        for w in range(2 * own)
        for i in range(CUTS)
    ]
    tokens_copy(0).start()
    for copy in small + weight_copies:
        copy.start()
    for i in range(1, many):
        tokens_copy(i).start()
    for copy in small:
        copy.wait()
    count = counts[lax.axis_index("seq")]

    def group(i, _):
        first = pl.multiple_of(i * size, size)
        tokens_copy(i).wait()
        values = tokens[pl.ds(first, size)].reshape(size * STEPS, D)
        normed = rms(values, gains[0:1, :])

        @pl.when(i == 0)
        def _():
            for copy in weight_copies:
                copy.wait()
            for source, target, sem in zip(later_hbm, later, range(extra)):
                pltpu.make_async_copy(source, target, later_sems.at[sem]).start()

        @pl.when(base + first < count)
        def _():
            after = time_group(values, normed, *weights, ctx)
            x1[pl.ds(first, size)] = after.reshape(size, STEPS, D)

        @pl.when(base + first >= count)
        def _():
            x1[pl.ds(first, size)] = jnp.zeros((size, STEPS, D), BF16)

        return 0

    lax.fori_loop(0, many, group, 0)
    turn = regroup(slots)
    for part in range(STEPS // 16):
        rows = x1[:, part * 16 : (part + 1) * 16, :].reshape(slots * 16, D)
        turned = dot(turn, rows).astype(BF16)
        span = 16 // LOCAL
        result[part * span : (part + 1) * span] = turned.reshape(span, LOCAL * slots, D)
    for source, target, sem in zip(later_hbm, later, range(extra)):
        pltpu.make_async_copy(source, target, later_sems.at[sem]).wait()


def time_part(base, slots, size, arrays, weights, own=True, keep=False, later=()):
    vmem = pl.BlockSpec(memory_space=pltpu.VMEM)
    hbm = pl.BlockSpec(memory_space=pltpu.HBM)
    extra = len(later)
    pin = lambda xs: [pltpu.with_memory_space_constraint(x, pltpu.HBM) for x in xs]
    like = lambda xs: [jax.ShapeDtypeStruct(x.shape, x.dtype) for x in xs]
    given = [] if keep or not own else [pltpu.VMEM(x.shape, x.dtype) for x in weights]
    result, *others = pl.pallas_call(
        functools.partial(time_kernel, base, size, own, keep, extra),
        in_specs=[hbm] * 3 + [hbm if own else vmem] * 2 + [hbm] * extra,
        out_specs=[vmem] * (1 + 2 * keep + extra),
        out_shape=[jax.ShapeDtypeStruct((GROUPS, LOCAL * slots, D), BF16)]
        + (like(weights) if keep else [])
        + like(later),
        scratch_shapes=[
            pltpu.SMEM((GROUPS,), jnp.int32),
            pltpu.VMEM((3, D), F32),
            pltpu.VMEM((slots, STEPS, D), BF16),
            *given,
            pltpu.VMEM((slots, STEPS, D), BF16),
            pltpu.VMEM((size * STEPS, D), BF16),
            pltpu.SemaphoreType.DMA((2,)),
            pltpu.SemaphoreType.DMA((slots // size,)),
            pltpu.SemaphoreType.DMA((2 * CUTS,)),
            pltpu.SemaphoreType.DMA((max(extra, 1),)),
        ],
        compiler_params=pltpu.CompilerParams(vmem_limit_bytes=32 << 20),
        cost_estimate=pl.CostEstimate(
            flops=slots * (6 << 26), bytes_accessed=4 << 20, transcendentals=slots << 16
        ),
        name=f"time_part_{base}_{slots}",
    )(*pin(arrays), *(pin(weights) if own else weights), *pin(later))
    return result, others


def mlp_rows(x1, o2, gains, in_w, back_w):
    x2 = (x1.astype(F32) + o2.astype(F32)).astype(BF16)
    hidden = jnp.maximum(dot(rms(x2, gains[2:3, :]), in_w[...]), 0.0).astype(BF16)
    return (x2.astype(F32) + dot(hidden, back_w[...])).astype(BF16)


def scene_kernel(parts, mlp, fetch, counts, *refs):
    many, end = len(parts), len(parts) + 7 + 2 * mlp
    recv, (gains, *weights, result, xs, packed, ctx) = refs[:many], refs[many:end]
    copies = []
    if fetch:
        *targets, sems = refs[end:]
        sources, weights = weights[-fetch:], weights[:-fetch] + targets
        copies = [
            pltpu.make_async_copy(source, target, sems.at[i])
            for i, (source, target) in enumerate(zip(sources, targets))
        ]
    for copy in copies:
        copy.start()
    qkv_w, out_w = weights[:2]
    offsets, offset = [], jnp.int32(0)
    for block in range(GROUPS):
        offsets.append((offset, counts[block]))
        offset = offset + counts[block]

    def places(block_of, slot):
        start, count = jnp.zeros_like(block_of), jnp.zeros_like(block_of)
        for block, (first, live) in enumerate(offsets):
            mine = block_of == block
            start = jnp.where(mine, first, start)
            count = jnp.where(mine, live, count)
        return jnp.where(slot < count, slot + start, -1)

    def gather(place):
        return jnp.where(iota((LIVE, place.shape[1]), 0) == place[0:1], 1.0, 0.0).astype(BF16)

    if many == 1:
        column = iota((8, AGENTS), 1)
        whole = gather(places(column >> 4, column & 15))
        for local in range(LOCAL):
            x = recv[0][:, local * SLOTS : (local + 1) * SLOTS, :].reshape(AGENTS, D)
            xs[local * LIVE : (local + 1) * LIVE] = dot(whole, x).astype(BF16)
    else:
        placed = []
        for base, slots in parts:
            width = LOCAL * slots
            column = iota((8, GROUPS * width), 1)
            block_of = (column * (65536 // width + 1)) >> 16
            row = column - block_of * width
            local_of = jnp.where(row < slots, 0, 1)
            place = places(block_of, base + row - local_of * slots)
            placed.append((place, local_of))
        for local in range(LOCAL):
            x = 0.0
            for ref, (place, local_of) in zip(recv, placed):
                pick = gather(jnp.where(local_of == local, place, -1))
                x = x + dot(pick, ref[...].reshape(pick.shape[1], D))
            xs[local * LIVE : (local + 1) * LIVE] = x.astype(BF16)

    blocks = [slice(i * LIVE, (i + 1) * LIVE) for i in range(LOCAL)]
    for rows in blocks:
        packed[rows] = dot(rms(xs[rows], gains[1:2, :]), qkv_w[...]).astype(BF16)
    for rows in blocks:
        for low in range(0, D, QUAD):
            q = packed[rows, low : low + QUAD]
            k = packed[rows, D + low : D + low + QUAD]
            v = packed[rows, 2 * D + low : 2 * D + low + QUAD]
            ctx[rows, low : low + QUAD] = scene_quad(q, k, v)

    for copy in copies:
        copy.wait()
    lane = iota((SLOTS, LIVE), 1) - iota((SLOTS, LIVE), 0)
    row = iota((SLOTS, LIVE), 0)
    scatter = jnp.concatenate(
        [
            jnp.where((lane == start) & (row < count), 1.0, 0.0).astype(BF16)
            for start, count in offsets
        ],
        axis=0,
    )
    for i, rows in enumerate(blocks):
        o2 = dot(ctx[rows], out_w[...]).astype(BF16)
        encoded = mlp_rows(xs[rows], o2, gains, *weights[2:]) if mlp else o2
        spread = dot(scatter, encoded).astype(BF16)
        result[:, i * SLOTS : (i + 1) * SLOTS, :] = spread.reshape(GROUPS, SLOTS, D)


def scene_part(parts, recv, counts, gains, weights, fetch):
    vmem = pl.BlockSpec(memory_space=pltpu.VMEM)
    hbm = pl.BlockSpec(memory_space=pltpu.HBM)
    scratch = [
        pltpu.VMEM((LOCAL * LIVE, D), BF16),
        pltpu.VMEM((LOCAL * LIVE, 3 * D), BF16),
        pltpu.VMEM((LOCAL * LIVE, D), BF16),
    ]
    mlp, now = len(weights) == 4, len(weights) - fetch
    weights, later = list(weights[:now]), weights[now:]
    for x in later:
        weights.append(pltpu.with_memory_space_constraint(x, pltpu.HBM))
        scratch.append(pltpu.VMEM(x.shape, x.dtype))
    if fetch:
        scratch.append(pltpu.SemaphoreType.DMA((fetch,)))
    specs = [pl.BlockSpec(memory_space=pltpu.SMEM)] + [vmem] * (len(recv) + 1 + now)
    return pl.pallas_call(
        functools.partial(scene_kernel, parts, mlp, fetch),
        in_specs=specs + [hbm] * fetch,
        out_specs=vmem,
        out_shape=jax.ShapeDtypeStruct((GROUPS, LOCAL * SLOTS, D), BF16),
        scratch_shapes=scratch,
        compiler_params=pltpu.CompilerParams(vmem_limit_bytes=40 << 20),
        cost_estimate=pl.CostEstimate(
            flops=10 << 30, bytes_accessed=8 << 20, transcendentals=2 << 20
        ),
        name=f"scene_part_{len(parts)}",
    )(counts, *recv, gains, *weights)


def mlp_kernel(counts, x1, o2, gains, in_w, back_w, result):
    count = counts[lax.axis_index("seq")]
    span = 16 // LOCAL

    def part(i, _):
        here = pl.ds(pl.multiple_of(i * span, span), span)
        rows = (span * LOCAL * SLOTS, D)
        encoded = mlp_rows(x1[here].reshape(rows), o2[here].reshape(rows), gains, in_w, back_w)
        live = (iota(rows, 0) & (SLOTS - 1)) < count
        encoded = jnp.where(live, encoded.astype(F32), 0.0).astype(BF16)
        result[here] = encoded.reshape(span, LOCAL * SLOTS, D)
        return 0

    lax.fori_loop(0, GROUPS // span, part, 0)


def mlp_part(counts, x1, o2, gains, in_w, back_w):
    vmem = pl.BlockSpec(memory_space=pltpu.VMEM)
    return pl.pallas_call(
        mlp_kernel,
        in_specs=[pl.BlockSpec(memory_space=pltpu.SMEM)] + [vmem] * 5,
        out_specs=vmem,
        out_shape=jax.ShapeDtypeStruct((GROUPS, LOCAL * SLOTS, D), BF16),
        compiler_params=pltpu.CompilerParams(vmem_limit_bytes=24 << 20),
        cost_estimate=pl.CostEstimate(flops=4 << 30, bytes_accessed=6 << 20, transcendentals=0),
        name="mlp_part",
    )(counts, x1, o2, gains, in_w, back_w)


def order_kernel(recv, result, turned, sems):
    turn = regroup(SLOTS)
    span = 16 // LOCAL
    copies = []
    for part in range(STEPS // 16):
        rows = recv[part * span : (part + 1) * span].reshape(256, D)
        turned[part] = dot(turn, rows).astype(BF16).reshape(SLOTS, 16, D)
        copies.append(
            pltpu.make_async_copy(
                turned.at[part], result.at[:, pl.ds(part * 16, 16), :], sems.at[part]
            )
        )
        copies[-1].start()
    for copy in copies:
        copy.wait()


def order_part(recv):
    return pl.pallas_call(
        order_kernel,
        in_specs=[pl.BlockSpec(memory_space=pltpu.VMEM)],
        out_specs=pl.BlockSpec(memory_space=pltpu.HBM),
        out_shape=jax.ShapeDtypeStruct((SLOTS, STEPS, D), BF16),
        scratch_shapes=[
            pltpu.VMEM((STEPS // 16, SLOTS, 16, D), BF16),
            pltpu.SemaphoreType.DMA((STEPS // 16,)),
        ],
        compiler_params=pltpu.CompilerParams(vmem_limit_bytes=16 << 20),
        name="order_part",
    )(recv)


def exchange(values):
    return lax.all_to_all(values, "seq", split_axis=0, concat_axis=0, tiled=True)


def one_exchange(counts, tokens, gains, qkv_time, out_time, *later):
    arrays, weights = (counts, tokens, gains), (qkv_time, out_time)
    after_time, fetched = time_part(0, SLOTS, 8, arrays, weights, later=later[:2])
    recv = [exchange(after_time)]
    o2 = exchange(scene_part([(0, SLOTS)], recv, counts, gains, fetched, 0))
    return mlp_part(counts, after_time, o2, gains, *later[2:])


def two_exchanges(counts, tokens, gains, qkv_time, out_time, *later):
    arrays, weights = (counts, tokens, gains), (qkv_time, out_time)
    parts = [(0, EARLY), (EARLY, SLOTS - EARLY)]
    early, kept = time_part(*parts[0], EARLY, arrays, weights, keep=KEEP)
    late, fetched = time_part(
        *parts[1], LATE_SIZE, arrays, kept or weights, own=not KEEP, later=later[:2]
    )
    recv = [exchange(early), exchange(late)]
    return exchange(scene_part(parts, recv, counts, gains, (*fetched, *later[2:]), 2))


def per_device(
    tokens, block_counts, gains, qkv_time, out_time, qkv_scene, out_scene, mlp_in, mlp_out
):
    returned = lax.cond(
        lax.axis_index("scene") % 2 == 0,
        one_exchange,
        two_exchanges,
        block_counts, tokens, gains, qkv_time, out_time, qkv_scene, out_scene, mlp_in, mlp_out,
    )
    return order_part(returned)


def solution(mesh):
    placed = (P(("scene", "seq"), None, None), P("scene"), P(), P(), P(), P(), P(), P(), P())
    return jax.shard_map(
        per_device,
        mesh=mesh,
        in_specs=placed,
        out_specs=P(("scene", "seq"), None, None),
        check_vma=False,
    )
```

```python
import functools

import jax
import jax.numpy as jnp
from jax import lax
from jax.experimental import pallas as pl
from jax.experimental.pallas import tpu as pltpu
from jax.sharding import PartitionSpec as P

D = 512
FF = 2048
SLOTS = 16
STEPS = 64
GROUPS = 32
LOCAL = STEPS // GROUPS
AGENTS = SLOTS * GROUPS
LIVE = 320
QUAD = 256
LANES = 128
LOWEST = -3e38
INV_ROOT = 0.125
EARLY = 4
BF16 = jnp.bfloat16
F32 = jnp.float32


def dot(a, b):
    return jnp.dot(a, b, preferred_element_type=F32)


def dot_nt(a, b):
    return lax.dot_general(a, b, (((1,), (1,)), ((), ())), preferred_element_type=F32)


def rms(values, gain):
    floats = values.astype(F32)
    inverse = lax.rsqrt(jnp.mean(floats * floats, axis=-1, keepdims=True) + 1e-06)
    return (floats * inverse * gain).astype(BF16)


def iota(shape, dim):
    return lax.broadcasted_iota(jnp.int32, shape, dim)


def regroup(slots):
    size = (slots * 16, slots * 16)
    row, col = iota(size, 0), iota(size, 1)
    return jnp.where(row == (col & 15) * slots + (col >> 4), 1.0, 0.0).astype(BF16)


def quad_masks(k):
    lane = iota(k.shape, 1) >> 6
    return jnp.concatenate([jnp.where(lane == h, k, jnp.zeros_like(k)) for h in range(4)], axis=0)


def time_group(values, normed, qkv_w, out_w, ctx, packed):
    agents = values.shape[0] // STEPS
    packed[...] = dot(normed, qkv_w[...]).astype(BF16)
    ones = quad_masks(jnp.ones((STEPS, QUAD), BF16))
    for agent in range(agents):
        rows = slice(agent * STEPS, (agent + 1) * STEPS)
        for low in range(0, D, QUAD):
            q = packed[rows, low : low + QUAD] * jnp.asarray(INV_ROOT, BF16)
            k = packed[rows, D + low : D + low + QUAD]
            v = packed[rows, 2 * D + low : 2 * D + low + QUAD]
            scores = dot_nt(q, quad_masks(k))
            p = []
            for half in range(0, QUAD, LANES):
                part = scores[:, half : half + LANES]
                left = iota(part.shape, 1) < STEPS
                top0 = jnp.max(jnp.where(left, part, LOWEST), axis=-1, keepdims=True)
                top1 = jnp.max(jnp.where(left, LOWEST, part), axis=-1, keepdims=True)
                p.append(jnp.exp(part - jnp.where(left, top0, top1)))
            p = jnp.concatenate(p, axis=1).astype(BF16)
            both = dot(p, jnp.concatenate([quad_masks(v), ones], axis=1))
            ctx[rows, low : low + QUAD] = (both[:, :QUAD] / both[:, QUAD:]).astype(BF16)
    update = dot(ctx[...], out_w[...])
    return (values.astype(F32) + update).astype(BF16)


def scene_quad(q, k, v):
    scores = dot_nt(q * jnp.asarray(INV_ROOT, BF16), quad_masks(k))
    p, inverse = [], []
    for low in range(0, 4 * LIVE, 2 * LIVE):
        a = scores[:, low : low + 256]
        m = scores[:, low + 256 : low + 384]
        b = scores[:, low + 384 : low + 640]
        left = iota(m.shape, 1) < 64
        top0 = jnp.maximum(a[:, :LANES], a[:, LANES:])
        top0 = jnp.max(jnp.maximum(top0, jnp.where(left, m, LOWEST)), axis=-1, keepdims=True)
        top1 = jnp.maximum(b[:, :LANES], b[:, LANES:])
        top1 = jnp.max(jnp.maximum(top1, jnp.where(left, LOWEST, m)), axis=-1, keepdims=True)
        a, b = jnp.exp(a - top0), jnp.exp(b - top1)
        m = jnp.exp(m - jnp.where(left, top0, top1))
        sum0 = a[:, :LANES] + a[:, LANES:] + jnp.where(left, m, 0.0)
        sum1 = b[:, :LANES] + b[:, LANES:] + jnp.where(left, 0.0, m)
        sum0 = jnp.sum(sum0, axis=-1, keepdims=True)
        sum1 = jnp.sum(sum1, axis=-1, keepdims=True)
        p += [a.astype(BF16), m.astype(BF16), b.astype(BF16)]
        inverse.append(1.0 / jnp.where(left, sum0, sum1))
    value = dot(jnp.concatenate(p, axis=1), quad_masks(v))
    return (value * jnp.concatenate(inverse, axis=1)).astype(BF16)


def time_kernel(base, size, extra, counts_hbm, tokens_hbm, gains_hbm, *refs):
    refs = list(refs)
    take = lambda many: [refs.pop(0) for _ in range(many)]
    sources, later_hbm, (result,) = take(2), take(extra), take(1)
    later, (counts, gains, tokens), weights = take(extra), take(3), take(2)
    x1, ctx, packed, sems, token_sems, weight_sems, later_sems = refs
    slots = tokens.shape[0]
    many = slots // size
    small = [
        pltpu.make_async_copy(counts_hbm, counts, sems.at[0]),
        pltpu.make_async_copy(gains_hbm, gains, sems.at[1]),
    ]

    def tokens_copy(i):
        first = pl.multiple_of(i * size, size)
        source = tokens_hbm.at[pl.ds(base + first, size)]
        return pltpu.make_async_copy(source, tokens.at[pl.ds(first, size)], token_sems.at[i])

    weight_copies = [
        pltpu.make_async_copy(sources[w], weights[w], weight_sems.at[w]) for w in range(2)
    ]

    tokens_copy(0).start()
    for copy in small + weight_copies:
        copy.start()
    for i in range(1, many):
        tokens_copy(i).start()
    for copy in small:
        copy.wait()
    count = counts[lax.axis_index("seq")]

    def group(i, _):
        first = pl.multiple_of(i * size, size)
        tokens_copy(i).wait()
        values = tokens[pl.ds(first, size)].reshape(size * STEPS, D)
        normed = rms(values, gains[0:1, :])

        @pl.when(i == 0)
        def _():
            for copy in weight_copies:
                copy.wait()
            for source, target, sem in zip(later_hbm, later, range(extra)):
                pltpu.make_async_copy(source, target, later_sems.at[sem]).start()

        @pl.when(base + first < count)
        def _():
            after = time_group(values, normed, *weights, ctx, packed)
            x1[pl.ds(first, size)] = after.reshape(size, STEPS, D)

        @pl.when(base + first >= count)
        def _():
            x1[pl.ds(first, size)] = jnp.zeros((size, STEPS, D), BF16)

        return 0

    lax.fori_loop(0, many, group, 0)
    turn = regroup(slots)
    for part in range(STEPS // 16):
        rows = x1[:, part * 16 : (part + 1) * 16, :].reshape(slots * 16, D)
        turned = dot(turn, rows).astype(BF16)
        span = 16 // LOCAL
        result[part * span : (part + 1) * span] = turned.reshape(span, LOCAL * slots, D)
    for source, target, sem in zip(later_hbm, later, range(extra)):
        pltpu.make_async_copy(source, target, later_sems.at[sem]).wait()


def time_part(base, slots, size, arrays, weights, later=()):
    vmem = pl.BlockSpec(memory_space=pltpu.VMEM)
    hbm = pl.BlockSpec(memory_space=pltpu.HBM)
    extra = len(later)
    pin = lambda xs: [pltpu.with_memory_space_constraint(x, pltpu.HBM) for x in xs]
    result, *others = pl.pallas_call(
        functools.partial(time_kernel, base, size, extra),
        in_specs=[hbm] * (5 + extra),
        out_specs=[vmem] * (1 + extra),
        out_shape=[jax.ShapeDtypeStruct((GROUPS, LOCAL * slots, D), BF16)]
        + [jax.ShapeDtypeStruct(x.shape, x.dtype) for x in later],
        scratch_shapes=[
            pltpu.SMEM((GROUPS,), jnp.int32),
            pltpu.VMEM((3, D), F32),
            pltpu.VMEM((slots, STEPS, D), BF16),
            *(pltpu.VMEM(x.shape, x.dtype) for x in weights),
            pltpu.VMEM((slots, STEPS, D), BF16),
            pltpu.VMEM((size * STEPS, D), BF16),
            pltpu.VMEM((size * STEPS, 3 * D), BF16),
            pltpu.SemaphoreType.DMA((2,)),
            pltpu.SemaphoreType.DMA((slots // size,)),
            pltpu.SemaphoreType.DMA((2,)),
            pltpu.SemaphoreType.DMA((max(extra, 1),)),
        ],
        compiler_params=pltpu.CompilerParams(vmem_limit_bytes=32 << 20),
        cost_estimate=pl.CostEstimate(
            flops=slots * (6 << 26), bytes_accessed=4 << 20, transcendentals=slots << 16
        ),
        name=f"time_part_{base}_{slots}",
    )(*pin(arrays), *pin(weights), *pin(later))
    return result, others


def mlp_rows(x1, o2, gains, in_w, back_w):
    x2 = (x1.astype(F32) + o2.astype(F32)).astype(BF16)
    hidden = jnp.maximum(dot(rms(x2, gains[2:3, :]), in_w[...]), 0.0).astype(BF16)
    return (x2.astype(F32) + dot(hidden, back_w[...])).astype(BF16)


def scene_kernel(parts, mlp, fetch, counts, *refs):
    many, end = len(parts), len(parts) + 7 + 2 * mlp
    recv, (gains, *weights, result, xs, packed, ctx) = refs[:many], refs[many:end]
    copies = []
    if fetch:
        *targets, sems = refs[end:]
        sources, weights = weights[-fetch:], weights[:-fetch] + targets
        copies = [
            pltpu.make_async_copy(source, target, sems.at[i])
            for i, (source, target) in enumerate(zip(sources, targets))
        ]
    for copy in copies:
        copy.start()
    qkv_w, out_w = weights[:2]
    offsets, offset = [], jnp.int32(0)
    for block in range(GROUPS):
        offsets.append((offset, counts[block]))
        offset = offset + counts[block]

    def places(block_of, slot):
        start, count = jnp.zeros_like(block_of), jnp.zeros_like(block_of)
        for block, (first, live) in enumerate(offsets):
            mine = block_of == block
            start = jnp.where(mine, first, start)
            count = jnp.where(mine, live, count)
        return jnp.where(slot < count, slot + start, -1)

    def gather(place):
        return jnp.where(iota((LIVE, place.shape[1]), 0) == place[0:1], 1.0, 0.0).astype(BF16)

    if many == 1:
        column = iota((8, AGENTS), 1)
        whole = gather(places(column >> 4, column & 15))
        for local in range(LOCAL):
            x = recv[0][:, local * SLOTS : (local + 1) * SLOTS, :].reshape(AGENTS, D)
            xs[local * LIVE : (local + 1) * LIVE] = dot(whole, x).astype(BF16)
    else:
        placed = []
        for base, slots in parts:
            width = LOCAL * slots
            column = iota((8, GROUPS * width), 1)
            block_of = (column * (65536 // width + 1)) >> 16
            row = column - block_of * width
            local_of = jnp.where(row < slots, 0, 1)
            place = places(block_of, base + row - local_of * slots)
            placed.append((place, local_of))
        for local in range(LOCAL):
            x = 0.0
            for ref, (place, local_of) in zip(recv, placed):
                pick = gather(jnp.where(local_of == local, place, -1))
                x = x + dot(pick, ref[...].reshape(pick.shape[1], D))
            xs[local * LIVE : (local + 1) * LIVE] = x.astype(BF16)

    blocks = [slice(i * LIVE, (i + 1) * LIVE) for i in range(LOCAL)]
    for rows in blocks:
        packed[rows] = dot(rms(xs[rows], gains[1:2, :]), qkv_w[...]).astype(BF16)
    for rows in blocks:
        for low in range(0, D, QUAD):
            q = packed[rows, low : low + QUAD]
            k = packed[rows, D + low : D + low + QUAD]
            v = packed[rows, 2 * D + low : 2 * D + low + QUAD]
            ctx[rows, low : low + QUAD] = scene_quad(q, k, v)

    lane = iota((SLOTS, LIVE), 1) - iota((SLOTS, LIVE), 0)
    row = iota((SLOTS, LIVE), 0)
    scatter = jnp.concatenate(
        [
            jnp.where((lane == start) & (row < count), 1.0, 0.0).astype(BF16)
            for start, count in offsets
        ],
        axis=0,
    )
    for i, rows in enumerate(blocks):
        o2 = dot(ctx[rows], out_w[...]).astype(BF16)
        if i == 0:
            for copy in copies:
                copy.wait()
        encoded = mlp_rows(xs[rows], o2, gains, *weights[2:]) if mlp else o2
        spread = dot(scatter, encoded).astype(BF16)
        result[:, i * SLOTS : (i + 1) * SLOTS, :] = spread.reshape(GROUPS, SLOTS, D)


def scene_part(parts, recv, counts, gains, weights, fetch):
    vmem = pl.BlockSpec(memory_space=pltpu.VMEM)
    hbm = pl.BlockSpec(memory_space=pltpu.HBM)
    scratch = [
        pltpu.VMEM((LOCAL * LIVE, D), BF16),
        pltpu.VMEM((LOCAL * LIVE, 3 * D), BF16),
        pltpu.VMEM((LOCAL * LIVE, D), BF16),
    ]
    mlp, now = len(weights) == 4, len(weights) - fetch
    weights, later = list(weights[:now]), weights[now:]
    for x in later:
        weights.append(pltpu.with_memory_space_constraint(x, pltpu.HBM))
        scratch.append(pltpu.VMEM(x.shape, x.dtype))
    if fetch:
        scratch.append(pltpu.SemaphoreType.DMA((fetch,)))
    specs = [pl.BlockSpec(memory_space=pltpu.SMEM)] + [vmem] * (len(recv) + 1 + now)
    return pl.pallas_call(
        functools.partial(scene_kernel, parts, mlp, fetch),
        in_specs=specs + [hbm] * fetch,
        out_specs=vmem,
        out_shape=jax.ShapeDtypeStruct((GROUPS, LOCAL * SLOTS, D), BF16),
        scratch_shapes=scratch,
        compiler_params=pltpu.CompilerParams(vmem_limit_bytes=40 << 20),
        cost_estimate=pl.CostEstimate(
            flops=10 << 30, bytes_accessed=8 << 20, transcendentals=2 << 20
        ),
        name=f"scene_part_{len(parts)}",
    )(counts, *recv, gains, *weights)


def mlp_kernel(counts, x1, o2, gains, in_w, back_w, result):
    count = counts[lax.axis_index("seq")]
    span = 16 // LOCAL

    def part(i, _):
        here = pl.ds(pl.multiple_of(i * span, span), span)
        rows = (span * LOCAL * SLOTS, D)
        encoded = mlp_rows(x1[here].reshape(rows), o2[here].reshape(rows), gains, in_w, back_w)
        live = (iota(rows, 0) & (SLOTS - 1)) < count
        encoded = jnp.where(live, encoded.astype(F32), 0.0).astype(BF16)
        result[here] = encoded.reshape(span, LOCAL * SLOTS, D)
        return 0

    lax.fori_loop(0, GROUPS // span, part, 0)


def mlp_part(counts, x1, o2, gains, in_w, back_w):
    vmem = pl.BlockSpec(memory_space=pltpu.VMEM)
    return pl.pallas_call(
        mlp_kernel,
        in_specs=[pl.BlockSpec(memory_space=pltpu.SMEM)] + [vmem] * 5,
        out_specs=vmem,
        out_shape=jax.ShapeDtypeStruct((GROUPS, LOCAL * SLOTS, D), BF16),
        compiler_params=pltpu.CompilerParams(vmem_limit_bytes=24 << 20),
        cost_estimate=pl.CostEstimate(flops=4 << 30, bytes_accessed=6 << 20, transcendentals=0),
        name="mlp_part",
    )(counts, x1, o2, gains, in_w, back_w)


def order_kernel(recv, result, turned, sems):
    turn = regroup(SLOTS)
    span = 16 // LOCAL
    copies = []
    for part in range(STEPS // 16):
        rows = recv[part * span : (part + 1) * span].reshape(256, D)
        turned[part] = dot(turn, rows).astype(BF16).reshape(SLOTS, 16, D)
        copies.append(
            pltpu.make_async_copy(
                turned.at[part], result.at[:, pl.ds(part * 16, 16), :], sems.at[part]
            )
        )
        copies[-1].start()
    for copy in copies:
        copy.wait()


def order_part(recv):
    return pl.pallas_call(
        order_kernel,
        in_specs=[pl.BlockSpec(memory_space=pltpu.VMEM)],
        out_specs=pl.BlockSpec(memory_space=pltpu.HBM),
        out_shape=jax.ShapeDtypeStruct((SLOTS, STEPS, D), BF16),
        scratch_shapes=[
            pltpu.VMEM((STEPS // 16, SLOTS, 16, D), BF16),
            pltpu.SemaphoreType.DMA((STEPS // 16,)),
        ],
        compiler_params=pltpu.CompilerParams(vmem_limit_bytes=16 << 20),
        name="order_part",
    )(recv)


def exchange(values):
    return lax.all_to_all(values, "seq", split_axis=0, concat_axis=0, tiled=True)


def one_exchange(counts, tokens, gains, qkv_time, out_time, *later):
    arrays, weights = (counts, tokens, gains), (qkv_time, out_time)
    after_time, fetched = time_part(0, SLOTS, 8, arrays, weights, later=later[:2])
    recv = [exchange(after_time)]
    o2 = exchange(scene_part([(0, SLOTS)], recv, counts, gains, fetched, 0))
    return mlp_part(counts, after_time, o2, gains, *later[2:])


def two_exchanges(counts, tokens, gains, qkv_time, out_time, *later):
    arrays, weights = (counts, tokens, gains), (qkv_time, out_time)
    parts = [(0, EARLY), (EARLY, SLOTS - EARLY)]
    early, _ = time_part(*parts[0], EARLY, arrays, weights)
    late, fetched = time_part(
        *parts[1], 4, arrays, weights, later=later[:2]
    )
    recv = [exchange(early), exchange(late)]
    return exchange(scene_part(parts, recv, counts, gains, (*fetched, *later[2:]), 2))


def per_device(
    tokens, block_counts, gains, qkv_time, out_time, qkv_scene, out_scene, mlp_in, mlp_out
):
    returned = lax.cond(
        lax.axis_index("scene") % 2 == 0,
        one_exchange,
        two_exchanges,
        block_counts, tokens, gains, qkv_time, out_time, qkv_scene, out_scene, mlp_in, mlp_out,
    )
    return order_part(returned)


def solution(mesh):
    placed = (P(("scene", "seq"), None, None), P("scene"), P(), P(), P(), P(), P(), P(), P())
    return jax.shard_map(
        per_device,
        mesh=mesh,
        in_specs=placed,
        out_specs=P(("scene", "seq"), None, None),
        check_vma=False,
    )
```

```python
import functools

import jax
import jax.numpy as jnp
from jax import lax
from jax.experimental import pallas as pl
from jax.experimental.pallas import tpu as pltpu
from jax.sharding import PartitionSpec as P

D = 512
FF = 2048
SLOTS = 16
STEPS = 64
GROUPS = 32
LOCAL = STEPS // GROUPS
AGENTS = SLOTS * GROUPS
LIVE = 320
QUAD = 256
LANES = 128
LOWEST = -3e38
INV_ROOT = 0.125
EARLY = 4
BF16 = jnp.bfloat16
F32 = jnp.float32


def dot(a, b):
    return jnp.dot(a, b, preferred_element_type=F32)


def dot_nt(a, b):
    return lax.dot_general(a, b, (((1,), (1,)), ((), ())), preferred_element_type=F32)


def rms(values, gain):
    floats = values.astype(F32)
    inverse = lax.rsqrt(jnp.mean(floats * floats, axis=-1, keepdims=True) + 1e-06)
    return (floats * inverse * gain).astype(BF16)


def iota(shape, dim):
    return lax.broadcasted_iota(jnp.int32, shape, dim)


def regroup(slots):
    size = (slots * 16, slots * 16)
    row, col = iota(size, 0), iota(size, 1)
    return jnp.where(row == (col & 15) * slots + (col >> 4), 1.0, 0.0).astype(BF16)


def quad_masks(k):
    lane = iota(k.shape, 1) >> 6
    return jnp.concatenate([jnp.where(lane == h, k, jnp.zeros_like(k)) for h in range(4)], axis=0)


def time_group(values, normed, qkv_w, out_w, ctx, packed):
    agents = values.shape[0] // STEPS
    packed[...] = dot(normed, qkv_w[...]).astype(BF16)
    ones = quad_masks(jnp.ones((STEPS, QUAD), BF16))
    for agent in range(agents):
        rows = slice(agent * STEPS, (agent + 1) * STEPS)
        for low in range(0, D, QUAD):
            q = packed[rows, low : low + QUAD] * jnp.asarray(INV_ROOT, BF16)
            k = packed[rows, D + low : D + low + QUAD]
            v = packed[rows, 2 * D + low : 2 * D + low + QUAD]
            scores = dot_nt(q, quad_masks(k))
            p = []
            for half in range(0, QUAD, LANES):
                part = scores[:, half : half + LANES]
                left = iota(part.shape, 1) < STEPS
                top0 = jnp.max(jnp.where(left, part, LOWEST), axis=-1, keepdims=True)
                top1 = jnp.max(jnp.where(left, LOWEST, part), axis=-1, keepdims=True)
                p.append(jnp.exp(part - jnp.where(left, top0, top1)))
            p = jnp.concatenate(p, axis=1).astype(BF16)
            both = dot(p, jnp.concatenate([quad_masks(v), ones], axis=1))
            ctx[rows, low : low + QUAD] = (both[:, :QUAD] / both[:, QUAD:]).astype(BF16)
    update = dot(ctx[...], out_w[...])
    return (values.astype(F32) + update).astype(BF16)


def scene_quad(q, k, v):
    scores = dot_nt(q * jnp.asarray(INV_ROOT, BF16), quad_masks(k))
    p, inverse = [], []
    for low in range(0, 4 * LIVE, 2 * LIVE):
        a = scores[:, low : low + 256]
        m = scores[:, low + 256 : low + 384]
        b = scores[:, low + 384 : low + 640]
        left = iota(m.shape, 1) < 64
        top0 = jnp.maximum(a[:, :LANES], a[:, LANES:])
        top0 = jnp.max(jnp.maximum(top0, jnp.where(left, m, LOWEST)), axis=-1, keepdims=True)
        top1 = jnp.maximum(b[:, :LANES], b[:, LANES:])
        top1 = jnp.max(jnp.maximum(top1, jnp.where(left, LOWEST, m)), axis=-1, keepdims=True)
        a, b = jnp.exp(a - top0), jnp.exp(b - top1)
        m = jnp.exp(m - jnp.where(left, top0, top1))
        sum0 = a[:, :LANES] + a[:, LANES:] + jnp.where(left, m, 0.0)
        sum1 = b[:, :LANES] + b[:, LANES:] + jnp.where(left, 0.0, m)
        sum0 = jnp.sum(sum0, axis=-1, keepdims=True)
        sum1 = jnp.sum(sum1, axis=-1, keepdims=True)
        p += [a.astype(BF16), m.astype(BF16), b.astype(BF16)]
        inverse.append(1.0 / jnp.where(left, sum0, sum1))
    value = dot(jnp.concatenate(p, axis=1), quad_masks(v))
    return (value * jnp.concatenate(inverse, axis=1)).astype(BF16)


def time_kernel(base, size, extra, counts_hbm, tokens_hbm, gains_hbm, *refs):
    refs = list(refs)
    take = lambda many: [refs.pop(0) for _ in range(many)]
    sources, later_hbm, (result,) = take(2), take(extra), take(1)
    later, (counts, gains, tokens), weights = take(extra), take(3), take(2)
    x1, ctx, packed, sems, token_sems, weight_sems, later_sems = refs
    slots = tokens.shape[0]
    many = slots // size
    small = [
        pltpu.make_async_copy(counts_hbm, counts, sems.at[0]),
        pltpu.make_async_copy(gains_hbm, gains, sems.at[1]),
    ]

    def tokens_copy(i):
        first = pl.multiple_of(i * size, size)
        source = tokens_hbm.at[pl.ds(base + first, size)]
        return pltpu.make_async_copy(source, tokens.at[pl.ds(first, size)], token_sems.at[i])

    weight_copies = [
        pltpu.make_async_copy(sources[w], weights[w], weight_sems.at[w]) for w in range(2)
    ]

    tokens_copy(0).start()
    for copy in small + weight_copies:
        copy.start()
    for i in range(1, many):
        tokens_copy(i).start()
    for copy in small:
        copy.wait()
    count = counts[lax.axis_index("seq")]

    def group(i, _):
        first = pl.multiple_of(i * size, size)
        tokens_copy(i).wait()
        values = tokens[pl.ds(first, size)].reshape(size * STEPS, D)
        normed = rms(values, gains[0:1, :])

        @pl.when(i == 0)
        def _():
            for copy in weight_copies:
                copy.wait()
            for source, target, sem in zip(later_hbm, later, range(extra)):
                pltpu.make_async_copy(source, target, later_sems.at[sem]).start()

        @pl.when(base + first < count)
        def _():
            after = time_group(values, normed, *weights, ctx, packed)
            x1[pl.ds(first, size)] = after.reshape(size, STEPS, D)

        @pl.when(base + first >= count)
        def _():
            x1[pl.ds(first, size)] = jnp.zeros((size, STEPS, D), BF16)

        return 0

    lax.fori_loop(0, many, group, 0)
    turn = regroup(slots)
    for part in range(STEPS // 16):
        rows = x1[:, part * 16 : (part + 1) * 16, :].reshape(slots * 16, D)
        turned = dot(turn, rows).astype(BF16)
        span = 16 // LOCAL
        result[part * span : (part + 1) * span] = turned.reshape(span, LOCAL * slots, D)
    for source, target, sem in zip(later_hbm, later, range(extra)):
        pltpu.make_async_copy(source, target, later_sems.at[sem]).wait()


def time_part(base, slots, size, arrays, weights, later=()):
    vmem = pl.BlockSpec(memory_space=pltpu.VMEM)
    hbm = pl.BlockSpec(memory_space=pltpu.HBM)
    extra = len(later)
    pin = lambda xs: [pltpu.with_memory_space_constraint(x, pltpu.HBM) for x in xs]
    result, *others = pl.pallas_call(
        functools.partial(time_kernel, base, size, extra),
        in_specs=[hbm] * (5 + extra),
        out_specs=[vmem] * (1 + extra),
        out_shape=[jax.ShapeDtypeStruct((GROUPS, LOCAL * slots, D), BF16)]
        + [jax.ShapeDtypeStruct(x.shape, x.dtype) for x in later],
        scratch_shapes=[
            pltpu.SMEM((GROUPS,), jnp.int32),
            pltpu.VMEM((3, D), F32),
            pltpu.VMEM((slots, STEPS, D), BF16),
            *(pltpu.VMEM(x.shape, x.dtype) for x in weights),
            pltpu.VMEM((slots, STEPS, D), BF16),
            pltpu.VMEM((size * STEPS, D), BF16),
            pltpu.VMEM((size * STEPS, 3 * D), BF16),
            pltpu.SemaphoreType.DMA((2,)),
            pltpu.SemaphoreType.DMA((slots // size,)),
            pltpu.SemaphoreType.DMA((2,)),
            pltpu.SemaphoreType.DMA((max(extra, 1),)),
        ],
        compiler_params=pltpu.CompilerParams(vmem_limit_bytes=32 << 20),
        cost_estimate=pl.CostEstimate(
            flops=slots * (6 << 26), bytes_accessed=4 << 20, transcendentals=slots << 16
        ),
        name=f"time_part_{base}_{slots}",
    )(*pin(arrays), *pin(weights), *pin(later))
    return result, others


def mlp_rows(x1, o2, gains, in_w, back_w):
    x2 = (x1.astype(F32) + o2.astype(F32)).astype(BF16)
    hidden = jnp.maximum(dot(rms(x2, gains[2:3, :]), in_w[...]), 0.0).astype(BF16)
    return (x2.astype(F32) + dot(hidden, back_w[...])).astype(BF16)


def scene_kernel(parts, mlp, fetch, counts, *refs):
    many, end = len(parts), len(parts) + 7 + 2 * mlp
    recv, (gains, *weights, result, xs, packed, ctx) = refs[:many], refs[many:end]
    copies = []
    if fetch:
        *targets, sems = refs[end:]
        sources, weights = weights[-fetch:], weights[:-fetch] + targets
        copies = [
            pltpu.make_async_copy(source, target, sems.at[i])
            for i, (source, target) in enumerate(zip(sources, targets))
        ]
    for copy in copies:
        copy.start()
    qkv_w, out_w = weights[:2]
    offsets, offset = [], jnp.int32(0)
    for block in range(GROUPS):
        offsets.append((offset, counts[block]))
        offset = offset + counts[block]

    def places(block_of, slot):
        start, count = jnp.zeros_like(block_of), jnp.zeros_like(block_of)
        for block, (first, live) in enumerate(offsets):
            mine = block_of == block
            start = jnp.where(mine, first, start)
            count = jnp.where(mine, live, count)
        return jnp.where(slot < count, slot + start, -1)

    def gather(place):
        return jnp.where(iota((LIVE, place.shape[1]), 0) == place[0:1], 1.0, 0.0).astype(BF16)

    if many == 1:
        column = iota((8, AGENTS), 1)
        whole = gather(places(column >> 4, column & 15))
        for local in range(LOCAL):
            x = recv[0][:, local * SLOTS : (local + 1) * SLOTS, :].reshape(AGENTS, D)
            xs[local * LIVE : (local + 1) * LIVE] = dot(whole, x).astype(BF16)
    else:
        placed = []
        for base, slots in parts:
            width = LOCAL * slots
            column = iota((8, GROUPS * width), 1)
            block_of = (column * (65536 // width + 1)) >> 16
            row = column - block_of * width
            local_of = jnp.where(row < slots, 0, 1)
            place = places(block_of, base + row - local_of * slots)
            placed.append((place, local_of))
        for local in range(LOCAL):
            x = 0.0
            for ref, (place, local_of) in zip(recv, placed):
                pick = gather(jnp.where(local_of == local, place, -1))
                x = x + dot(pick, ref[...].reshape(pick.shape[1], D))
            xs[local * LIVE : (local + 1) * LIVE] = x.astype(BF16)

    blocks = [slice(i * LIVE, (i + 1) * LIVE) for i in range(LOCAL)]
    for rows in blocks:
        packed[rows] = dot(rms(xs[rows], gains[1:2, :]), qkv_w[...]).astype(BF16)
    for rows in blocks:
        for low in range(0, D, QUAD):
            q = packed[rows, low : low + QUAD]
            k = packed[rows, D + low : D + low + QUAD]
            v = packed[rows, 2 * D + low : 2 * D + low + QUAD]
            ctx[rows, low : low + QUAD] = scene_quad(q, k, v)

    lane = iota((SLOTS, LIVE), 1) - iota((SLOTS, LIVE), 0)
    row = iota((SLOTS, LIVE), 0)
    scatter = jnp.concatenate(
        [
            jnp.where((lane == start) & (row < count), 1.0, 0.0).astype(BF16)
            for start, count in offsets
        ],
        axis=0,
    )
    for i, rows in enumerate(blocks):
        o2 = dot(ctx[rows], out_w[...]).astype(BF16)
        if i == 0:
            for copy in copies:
                copy.wait()
        encoded = mlp_rows(xs[rows], o2, gains, *weights[2:]) if mlp else o2
        spread = dot(scatter, encoded).astype(BF16)
        result[:, i * SLOTS : (i + 1) * SLOTS, :] = spread.reshape(GROUPS, SLOTS, D)


def scene_part(parts, recv, counts, gains, weights, fetch):
    vmem = pl.BlockSpec(memory_space=pltpu.VMEM)
    hbm = pl.BlockSpec(memory_space=pltpu.HBM)
    scratch = [
        pltpu.VMEM((LOCAL * LIVE, D), BF16),
        pltpu.VMEM((LOCAL * LIVE, 3 * D), BF16),
        pltpu.VMEM((LOCAL * LIVE, D), BF16),
    ]
    mlp, now = len(weights) == 4, len(weights) - fetch
    weights, later = list(weights[:now]), weights[now:]
    for x in later:
        weights.append(pltpu.with_memory_space_constraint(x, pltpu.HBM))
        scratch.append(pltpu.VMEM(x.shape, x.dtype))
    if fetch:
        scratch.append(pltpu.SemaphoreType.DMA((fetch,)))
    specs = [pl.BlockSpec(memory_space=pltpu.SMEM)] + [vmem] * (len(recv) + 1 + now)
    return pl.pallas_call(
        functools.partial(scene_kernel, parts, mlp, fetch),
        in_specs=specs + [hbm] * fetch,
        out_specs=vmem,
        out_shape=jax.ShapeDtypeStruct((GROUPS, LOCAL * SLOTS, D), BF16),
        scratch_shapes=scratch,
        compiler_params=pltpu.CompilerParams(vmem_limit_bytes=40 << 20),
        cost_estimate=pl.CostEstimate(
            flops=10 << 30, bytes_accessed=8 << 20, transcendentals=2 << 20
        ),
        name=f"scene_part_{len(parts)}",
    )(counts, *recv, gains, *weights)


def mlp_kernel(counts, x1, o2, gains, in_w, back_w, result):
    count = counts[lax.axis_index("seq")]
    span = 16 // LOCAL

    def part(i, _):
        here = pl.ds(pl.multiple_of(i * span, span), span)
        rows = (span * LOCAL * SLOTS, D)
        encoded = mlp_rows(x1[here].reshape(rows), o2[here].reshape(rows), gains, in_w, back_w)
        live = (iota(rows, 0) & (SLOTS - 1)) < count
        encoded = jnp.where(live, encoded.astype(F32), 0.0).astype(BF16)
        result[here] = encoded.reshape(span, LOCAL * SLOTS, D)
        return 0

    lax.fori_loop(0, GROUPS // span, part, 0)


def mlp_part(counts, x1, o2, gains, in_w, back_w):
    vmem = pl.BlockSpec(memory_space=pltpu.VMEM)
    return pl.pallas_call(
        mlp_kernel,
        in_specs=[pl.BlockSpec(memory_space=pltpu.SMEM)] + [vmem] * 5,
        out_specs=vmem,
        out_shape=jax.ShapeDtypeStruct((GROUPS, LOCAL * SLOTS, D), BF16),
        compiler_params=pltpu.CompilerParams(vmem_limit_bytes=24 << 20),
        cost_estimate=pl.CostEstimate(flops=4 << 30, bytes_accessed=6 << 20, transcendentals=0),
        name="mlp_part",
    )(counts, x1, o2, gains, in_w, back_w)


def order_kernel(recv, result, turned, sems):
    turn = regroup(SLOTS)
    span = 16 // LOCAL
    copies = []
    for part in range(STEPS // 16):
        rows = recv[part * span : (part + 1) * span].reshape(256, D)
        turned[part] = dot(turn, rows).astype(BF16).reshape(SLOTS, 16, D)
        copies.append(
            pltpu.make_async_copy(
                turned.at[part], result.at[:, pl.ds(part * 16, 16), :], sems.at[part]
            )
        )
        copies[-1].start()
    for copy in copies:
        copy.wait()


def order_part(recv):
    return pl.pallas_call(
        order_kernel,
        in_specs=[pl.BlockSpec(memory_space=pltpu.VMEM)],
        out_specs=pl.BlockSpec(memory_space=pltpu.HBM),
        out_shape=jax.ShapeDtypeStruct((SLOTS, STEPS, D), BF16),
        scratch_shapes=[
            pltpu.VMEM((STEPS // 16, SLOTS, 16, D), BF16),
            pltpu.SemaphoreType.DMA((STEPS // 16,)),
        ],
        compiler_params=pltpu.CompilerParams(vmem_limit_bytes=16 << 20),
        name="order_part",
    )(recv)


def exchange(values):
    return lax.all_to_all(values, "seq", split_axis=0, concat_axis=0, tiled=True)


def one_exchange(counts, tokens, gains, qkv_time, out_time, *later):
    arrays, weights = (counts, tokens, gains), (qkv_time, out_time)
    after_time, fetched = time_part(0, SLOTS, 16, arrays, weights, later=later[:2])
    recv = [exchange(after_time)]
    o2 = exchange(scene_part([(0, SLOTS)], recv, counts, gains, fetched, 0))
    return mlp_part(counts, after_time, o2, gains, *later[2:])


def two_exchanges(counts, tokens, gains, qkv_time, out_time, *later):
    arrays, weights = (counts, tokens, gains), (qkv_time, out_time)
    parts = [(0, EARLY), (EARLY, SLOTS - EARLY)]
    early, _ = time_part(*parts[0], EARLY, arrays, weights)
    late, fetched = time_part(
        *parts[1], 4, arrays, weights, later=later[:2]
    )
    recv = [exchange(early), exchange(late)]
    return exchange(scene_part(parts, recv, counts, gains, (*fetched, *later[2:]), 2))


def per_device(
    tokens, block_counts, gains, qkv_time, out_time, qkv_scene, out_scene, mlp_in, mlp_out
):
    returned = lax.cond(
        lax.axis_index("scene") % 2 == 0,
        one_exchange,
        two_exchanges,
        block_counts, tokens, gains, qkv_time, out_time, qkv_scene, out_scene, mlp_in, mlp_out,
    )
    return order_part(returned)


def solution(mesh):
    placed = (P(("scene", "seq"), None, None), P("scene"), P(), P(), P(), P(), P(), P(), P())
    return jax.shard_map(
        per_device,
        mesh=mesh,
        in_specs=placed,
        out_specs=P(("scene", "seq"), None, None),
        check_vma=False,
    )
```
